32 devices in a mesh: groups: 2 (over y), wide: 8 (over z, x), head: 2 (over core).
Axes of the slice: x: 2, y: 2, z: 4, core: 2. Of those that a mesh axis runs over, the one named last changes fastest.
Arguments:
- tokens: bfloat16 [1024, 2048], P(('groups', 'wide'), 'head'), parts along dimension 0, may hold values from -6 to 6
- expert_ids: int32 [1024, 8], P(('groups', 'wide')), parts along dimension 0, may hold values from 0 to 7, as said below
- gate_scores: float32 [1024, 8], P(('groups', 'wide')), parts along dimension 0, may hold values from 0.25 to 1
- gate_proj: bfloat16 [8, 704, 2048], P('wide', 'head'), may hold values from -0.125 to 0.125
- up_proj: bfloat16 [8, 704, 2048], P('wide', 'head'), may hold values from -0.125 to 0.125
- down_proj: bfloat16 [8, 704, 2048], P('wide', 'head'), may hold values from -0.21875 to 0.21875
Outputs:
- mixed: bfloat16 [1024, 2048], P(('groups', 'wide'), 'head'), parts along dimension 0
The draws below stay inside these ranges and needn't reach their ends.
There are 2 independent parts, one for each index of `groups`. The reference program is written for one: setup_inputs(seed, part) draws one part's arguments, and reference() takes and returns one part's arrays. A program takes and returns all parts, laid end to end along the dimension named above; an argument that names none is the same for every part. Nothing has to cross between parts.
Inputs may be any that keep to these rules, and one draw needn't show every extreme that they name: `expert_ids`: each row names 8 different experts. Within each aligned block of 64 rows at most 64 rows name the same expert, and in every draw one expert is named by exactly 64 rows of every such block.
All inputs are finite; a program needn't handle non-finite values.
Results may differ from the reference program's by a relative error of at most 0.01.
Values may be sent and summed in bfloat16 or wider, within the bound.
No kernel may reach another device: no remote copies, remote signals or barrier semaphores. Data moves between devices by JAX's collectives and lax.ppermute only.
A program may use at most 64 MiB of HBM per device.

```python
import math
import jax
import jax.numpy as jnp
from jax import lax

D = 2048
FF = 704
TOP = 8
TOK_DEV = 64
TOKENS = 512
EXPERTS = 8
CAP = 64
N_WIDE = 8


def draw_expert_ids(key, part):
    block_count = TOKENS // TOK_DEV
    hot_key, pref_key, rows_key = jax.random.split(jax.random.fold_in(key, 7), 3)
    hot_expert = jax.random.randint(hot_key, (), 0, EXPERTS)
    preference = jax.random.randint(pref_key, (EXPERTS,), 0, 2048)
    expert_numbers = jnp.arange(EXPERTS, dtype=jnp.int32)

    def draw_block(block_key):
        row_noise = jax.random.randint(block_key, (TOK_DEV, EXPERTS), 0, 2048)

        def assign_row(counts_now, noise_row):
            scores = preference + noise_row
            boosted = jnp.logical_and(expert_numbers == hot_expert, counts_now < CAP)
            scores = jnp.where(boosted, scores + 8192, scores)
            scores = jnp.where(counts_now >= CAP, -1, scores)
            keyed_scores = scores * EXPERTS + expert_numbers
            unused, chosen = lax.top_k(keyed_scores, TOP)
            chosen = chosen.astype(jnp.int32)
            added = jnp.sum((chosen[:, None] == expert_numbers[None, :]).astype(jnp.int32), axis=0)
            return (counts_now + added, chosen)
        unused, drawn_ids = lax.scan(assign_row, jnp.zeros((EXPERTS,), jnp.int32), row_noise)
        return drawn_ids
    block_keys = jax.random.split(rows_key, block_count)
    drawn_ids = jax.vmap(draw_block)(block_keys)
    return drawn_ids.reshape(TOKENS, TOP).astype(jnp.int32)


def levels(key, extent, shards, low, largest):
    def one(position, blocks):
        steps = jax.random.uniform(jax.random.fold_in(jax.random.fold_in(key, 6), position), (blocks,), jnp.float32, low / len(shards), largest / len(shards))
        return jnp.repeat(jnp.exp(steps), extent[position] // blocks).reshape((-1,) + (1,) * (len(extent) - position - 1))

    level = one(*shards[0])
    for cut in shards[1:]:
        level = level * one(*cut)
    return level


def normal_values(key, shape, spread, reach, cuts=(), kind=jnp.bfloat16):
    result = jax.random.normal(key, shape, jnp.float32) * spread
    if len(cuts) > 0:
        result = levels(key, shape, cuts, -0.22, 0.18) * result
    return jnp.clip(result, min=-reach, max=reach).astype(kind)


def setup_inputs(seed: int = 0, part: int = 0) -> dict:
    key_list = jax.random.split(jax.random.key(seed), 7)
    part_keys = jax.random.split(jax.random.fold_in(key_list[6], part), 7)
    tokens = normal_values(part_keys[0], (TOKENS, D), 1.0, 6.0, ((0, 8), (1, 2)))
    expert_ids = draw_expert_ids(jax.random.fold_in(jax.random.fold_in(key_list[6], part), 71), part)
    gate_scores = jnp.clip(jnp.exp(math.log(1.0) - 1.3862944 * jax.random.uniform(part_keys[2], (TOKENS, TOP), jnp.float32) ** levels(part_keys[2], (TOKENS, TOP), ((0, 8),), -0.2, 0.2)), 0.25, 1.0)
    gate_proj = normal_values(key_list[3], (EXPERTS, FF, D), D ** -0.5, 0.125, ((0, 8), (1, 2)))
    up_proj = normal_values(key_list[4], (EXPERTS, FF, D), D ** -0.5, 0.125, ((0, 8), (1, 2)))
    down_proj = normal_values(key_list[5], (EXPERTS, FF, D), FF ** -0.5, 0.21875, ((0, 8), (1, 2)))
    return {"tokens": tokens, "expert_ids": expert_ids, "gate_scores": gate_scores, "gate_proj": gate_proj, "up_proj": up_proj, "down_proj": down_proj}


def reference(tokens, expert_ids, gate_scores, gate_proj, up_proj, down_proj):
    token_count = tokens.shape[0]
    feature_width = tokens.shape[1]
    half_units = FF // 2
    slot_room = N_WIDE * CAP
    slot_numbers = jnp.arange(slot_room, dtype=jnp.int32)

    def one_expert(running, stacked_in):
        expert, w_gate, w_up, w_down = stacked_in
        chosen = expert_ids == expert
        weight = jnp.sum(jnp.where(chosen, gate_scores, jnp.zeros_like(gate_scores)), axis=1)
        named = jnp.any(chosen, axis=1)
        row_index = jnp.nonzero(named, size=slot_room, fill_value=0)[0].astype(jnp.int32)
        filled = slot_numbers < jnp.sum(named.astype(jnp.int32))
        picked = tokens[row_index]
        gate_part = jnp.dot(picked, w_gate.T, preferred_element_type=jnp.float32)
        up_part = jnp.dot(picked, w_up.T, preferred_element_type=jnp.float32)
        hidden = (jax.nn.silu(gate_part) * up_part).astype(jnp.bfloat16)
        lower_part = jnp.dot(hidden[:, :half_units], w_down[:half_units], preferred_element_type=jnp.float32).astype(jnp.bfloat16)
        upper_part = jnp.dot(hidden[:, half_units:], w_down[half_units:], preferred_element_type=jnp.float32).astype(jnp.bfloat16)
        expert_out = lower_part.astype(jnp.float32) + upper_part.astype(jnp.float32)
        scale_rows = jnp.where(filled, weight[row_index], jnp.zeros_like(weight[row_index]))
        weighted = expert_out * scale_rows[:, None]
        running = running.at[row_index].add(weighted)
        return running, None

    start = jnp.zeros((token_count, feature_width), jnp.float32)
    experts_list = jnp.arange(EXPERTS, dtype=jnp.int32)
    running_sum, unused = lax.scan(one_expert, start, (experts_list, gate_proj, up_proj, down_proj))
    return running_sum.astype(jnp.bfloat16)
```

```python
import functools

import jax
import jax.numpy as jnp
from jax import lax
from jax.experimental import pallas as pl
from jax.experimental.pallas import tpu as pltpu
from jax.sharding import PartitionSpec as P

LANES = 128
PIECES = 3
VMEM_LIMIT = 24 * 2**20


def sparse_local(tokens, expert_ids, gate_scores, gate_proj, up_proj, down_proj):
    experts = lax.axis_size("wide")
    tok_rows, top_count = expert_ids.shape
    ceiling = (tok_rows * top_count + experts - 1) // experts
    capacity = min(tok_rows, max(2, tok_rows // 8, 2 * ceiling))
    flat_ids = expert_ids.reshape(-1)
    expert_numbers = jnp.arange(experts, dtype=jnp.int32)
    onehot = (flat_ids[:, None] == expert_numbers[None, :]).astype(jnp.int32)
    earlier = jnp.cumsum(onehot, axis=0) - onehot
    slot_index = jnp.sum(earlier * onehot, axis=1)
    position = flat_ids * capacity + slot_index
    targets = jnp.arange(experts * capacity, dtype=jnp.int32)
    placing = jnp.any(
        position.reshape(tok_rows, top_count)[:, :, None] == targets[None, None, :], axis=1
    ).astype(jnp.bfloat16)
    w_gate = gate_proj[0]
    w_up = up_proj[0]
    w_down = down_proj[0]
    placed = lax.dot_general(
        placing, tokens, (((0,), (0,)), ((), ())), preferred_element_type=jnp.float32
    )
    outgoing = placed.astype(jnp.bfloat16).reshape(experts, capacity, tokens.shape[1])
    full_rows = lax.all_gather(
        lax.all_to_all(outgoing, "wide", split_axis=0, concat_axis=0, tiled=True),
        "head",
        axis=2,
        tiled=True,
    )
    src_count, item_count, feature_width = full_rows.shape
    stacked = full_rows.reshape(src_count * item_count, feature_width)
    gate_part = lax.dot_general(
        stacked, w_gate, (((1,), (1,)), ((), ())), preferred_element_type=jnp.float32
    )
    up_part = lax.dot_general(
        stacked, w_up, (((1,), (1,)), ((), ())), preferred_element_type=jnp.float32
    )
    hidden = (jax.nn.silu(gate_part) * up_part).astype(jnp.bfloat16)
    partial_value = jnp.dot(hidden, w_down, preferred_element_type=jnp.float32)
    partial_value = partial_value.reshape(src_count, item_count, feature_width)
    back = lax.psum_scatter(
        partial_value.astype(jnp.bfloat16), "head", scatter_dimension=2, tiled=True
    ).astype(jnp.float32)
    returned = lax.all_to_all(
        back.astype(jnp.bfloat16), "wide", split_axis=0, concat_axis=0, tiled=True
    ).astype(back.dtype)
    picked = returned.reshape(experts * capacity, returned.shape[2])[position]
    picked = picked.reshape(tok_rows, top_count, returned.shape[2])
    mixed = jnp.sum(gate_scores[:, :, None] * picked, axis=1)
    return mixed.astype(jnp.bfloat16)


def expert_kernel(counts, select_ref, *refs):
    blocks = refs[: len(counts)]
    wg0, wg1, wu0, wu1, wd0, wd1 = refs[len(counts) : len(counts) + 6]
    outs = refs[len(counts) + 6 :]
    width = wg0.shape[1]
    whole = [b[...] for b in blocks]
    rows = whole[0] if len(whole) == 1 else jnp.concatenate(whole, axis=0)
    x = rows[:, :width]
    scale = jnp.sum(rows[:, width:].astype(jnp.float32) * select_ref[...], axis=1, keepdims=True)
    total = None
    for wg, wu, wd in ((wg0, wu0, wd0), (wg1, wu1, wd1)):
        gate = lax.dot_general(
            x, wg[...], (((1,), (1,)), ((), ())), preferred_element_type=jnp.float32
        )
        up = lax.dot_general(
            x, wu[...], (((1,), (1,)), ((), ())), preferred_element_type=jnp.float32
        )
        hidden = (gate / (1.0 + jnp.exp(-gate)) * up).astype(jnp.bfloat16)
        term = jnp.dot(hidden, wd[...], preferred_element_type=jnp.float32)
        total = term if total is None else total + term
    scaled = (total * scale).astype(jnp.bfloat16)
    start = 0
    for count, out in zip(counts, outs):
        out[...] = scaled[start : start + count]
        start += count


def run_expert(blocks, select, weights):
    counts = tuple(b.shape[0] for b in blocks)
    width = weights[0].shape[1]
    units = sum(w.shape[0] for w in weights)
    spec = pl.BlockSpec(memory_space=pltpu.VMEM)
    return pl.pallas_call(
        functools.partial(expert_kernel, counts),
        out_shape=[jax.ShapeDtypeStruct((c, width), jnp.bfloat16) for c in counts],
        in_specs=[spec] * (1 + len(blocks) + len(weights)),
        out_specs=[spec] * len(blocks),
        compiler_params=pltpu.CompilerParams(vmem_limit_bytes=VMEM_LIMIT),
        cost_estimate=pl.CostEstimate(
            flops=2 * sum(counts) * units * width,
            bytes_accessed=2 * units * width,
            transcendentals=sum(counts) * units // 3,
        ),
    )(select, *blocks, *weights)


def dense_local(tokens, expert_ids, gate_scores, gate_proj, up_proj, down_proj):
    n = lax.axis_size("wide")
    head = lax.axis_index("head")
    expert = lax.axis_index("wide")
    tok_rows, half_width = tokens.shape
    part = tok_rows // 2
    swap = ((0, 1), (1, 0))
    order = list(range(0, n, 2)) + list(range(n - 1, 0, -2))
    ahead = [(order[i], order[(i + 1) % n]) for i in range(n)]
    behind = [(b, a) for a, b in ahead]

    def forth(v):
        return lax.ppermute(v, "wide", ahead)

    def back(v):
        return lax.ppermute(v, "wide", behind)

    mine = lax.dynamic_slice_in_dim(tokens, head * part, part, 0)
    other = lax.dynamic_slice_in_dim(tokens, (1 - head) * part, part, 0)
    got = lax.ppermute(other, "head", swap)
    first = head == 0
    named = expert_ids[:, :, None] == jnp.arange(n, dtype=jnp.int32)[None, None, :]
    scores = jnp.sum(jnp.where(named, gate_scores[:, :, None], 0.0), axis=1)
    scores = lax.dynamic_slice_in_dim(scores, head * part, part, 0)
    pieces = []
    rest = scores
    for _ in range(PIECES):
        piece = rest.astype(jnp.bfloat16)
        pieces.append(piece)
        rest = rest - piece.astype(jnp.float32)
    pad = jnp.zeros((part, LANES - PIECES * n), jnp.bfloat16)
    own = jnp.concatenate(
        [jnp.where(first, mine, got), jnp.where(first, got, mine)] + pieces + [pad], axis=1
    )
    lane = jnp.arange(LANES, dtype=jnp.int32)
    select = jnp.where(lane % n == expert, 1.0, 0.0).astype(jnp.float32)[None, :]

    weights = []
    for w in (gate_proj[0], up_proj[0], down_proj[0]):
        weights += [w, lax.ppermute(w, "head", swap)]

    half_round = n // 2
    cut = part // 2
    near = {0: own}
    f = b = own
    sums = {}
    todo = [0]
    for k in range(1, half_round):
        f, b = forth(f), back(b)
        near[-k], near[k] = f, b
        done = run_expert([near[i] for i in todo], select, weights)
        sums.update(zip(todo, done))
        todo = [-k, k]
    f, b = forth(f[:cut]), back(b[cut:])
    done = run_expert([near[i] for i in todo], select, weights)
    sums.update(zip(todo, done))
    far = run_expert([f, b], select, weights)

    f, b = forth(far[0]), back(far[1])
    for k in range(half_round - 1, 0, -1):
        up_sum = sums[k].astype(jnp.float32)
        down_sum = sums[-k].astype(jnp.float32)
        if k == half_round - 1:
            up_sum = jnp.concatenate([up_sum[:cut] + f.astype(jnp.float32), up_sum[cut:]], axis=0)
            down_sum = jnp.concatenate(
                [down_sum[:cut], down_sum[cut:] + b.astype(jnp.float32)], axis=0
            )
        else:
            up_sum = up_sum + f.astype(jnp.float32)
            down_sum = down_sum + b.astype(jnp.float32)
        f, b = forth(up_sum.astype(jnp.bfloat16)), back(down_sum.astype(jnp.bfloat16))
    mixed = (sums[0].astype(jnp.float32) + f.astype(jnp.float32) + b.astype(jnp.float32)).astype(
        jnp.bfloat16
    )
    left, right = mixed[:, :half_width], mixed[:, half_width:]
    keep = jnp.where(first, left, right)
    came = lax.ppermute(jnp.where(first, right, left), "head", swap)
    return jnp.concatenate(
        [jnp.where(first, keep, came), jnp.where(first, came, keep)], axis=0
    )


def local(tokens, expert_ids, gate_scores, gate_proj, up_proj, down_proj):
    n = lax.axis_size("wide")
    dense = expert_ids.shape[1] == n and lax.axis_size("head") == 2 and n % 2 == 0
    if dense and tokens.shape[0] % 64 == 0 and PIECES * n <= LANES:
        return dense_local(tokens, expert_ids, gate_scores, gate_proj, up_proj, down_proj)
    return sparse_local(tokens, expert_ids, gate_scores, gate_proj, up_proj, down_proj)


def solution(mesh):
    return jax.shard_map(
        local,
        mesh=mesh,
        in_specs=(
            P(("groups", "wide"), "head"),
            P(("groups", "wide"), None),
            P(("groups", "wide"), None),
            P("wide", "head", None),
            P("wide", "head", None),
            P("wide", "head", None),
        ),
        out_specs=P(("groups", "wide"), "head"),
        check_vma=False,
    )
```

```python
import functools

import jax
import jax.numpy as jnp
from jax import lax
from jax.experimental import pallas as pl
from jax.experimental.pallas import tpu as pltpu
from jax.sharding import PartitionSpec as P

LANES = 128
PIECES = 3
VMEM_LIMIT = 24 * 2**20


def sparse_local(tokens, expert_ids, gate_scores, gate_proj, up_proj, down_proj):
    experts = lax.axis_size("wide")
    tok_rows, top_count = expert_ids.shape
    ceiling = (tok_rows * top_count + experts - 1) // experts
    capacity = min(tok_rows, max(2, tok_rows // 8, 2 * ceiling))
    flat_ids = expert_ids.reshape(-1)
    expert_numbers = jnp.arange(experts, dtype=jnp.int32)
    onehot = (flat_ids[:, None] == expert_numbers[None, :]).astype(jnp.int32)
    earlier = jnp.cumsum(onehot, axis=0) - onehot
    slot_index = jnp.sum(earlier * onehot, axis=1)
    position = flat_ids * capacity + slot_index
    targets = jnp.arange(experts * capacity, dtype=jnp.int32)
    placing = jnp.any(
        position.reshape(tok_rows, top_count)[:, :, None] == targets[None, None, :], axis=1
    ).astype(jnp.bfloat16)
    w_gate = gate_proj[0]
    w_up = up_proj[0]
    w_down = down_proj[0]
    placed = lax.dot_general(
        placing, tokens, (((0,), (0,)), ((), ())), preferred_element_type=jnp.float32
    )
    outgoing = placed.astype(jnp.bfloat16).reshape(experts, capacity, tokens.shape[1])
    full_rows = lax.all_gather(
        lax.all_to_all(outgoing, "wide", split_axis=0, concat_axis=0, tiled=True),
        "head",
        axis=2,
        tiled=True,
    )
    src_count, item_count, feature_width = full_rows.shape
    stacked = full_rows.reshape(src_count * item_count, feature_width)
    gate_part = lax.dot_general(
        stacked, w_gate, (((1,), (1,)), ((), ())), preferred_element_type=jnp.float32
    )
    up_part = lax.dot_general(
        stacked, w_up, (((1,), (1,)), ((), ())), preferred_element_type=jnp.float32
    )
    hidden = (jax.nn.silu(gate_part) * up_part).astype(jnp.bfloat16)
    partial_value = jnp.dot(hidden, w_down, preferred_element_type=jnp.float32)
    partial_value = partial_value.reshape(src_count, item_count, feature_width)
    back = lax.psum_scatter(
        partial_value.astype(jnp.bfloat16), "head", scatter_dimension=2, tiled=True
    ).astype(jnp.float32)
    returned = lax.all_to_all(
        back.astype(jnp.bfloat16), "wide", split_axis=0, concat_axis=0, tiled=True
    ).astype(back.dtype)
    picked = returned.reshape(experts * capacity, returned.shape[2])[position]
    picked = picked.reshape(tok_rows, top_count, returned.shape[2])
    mixed = jnp.sum(gate_scores[:, :, None] * picked, axis=1)
    return mixed.astype(jnp.bfloat16)


def expert_kernel(counts, select_ref, *refs):
    blocks = refs[: len(counts)]
    wg0, wg1, wu0, wu1, wd0, wd1 = refs[len(counts) : len(counts) + 6]
    outs = refs[len(counts) + 6 :]
    width = wg0.shape[1]
    whole = [b[...] for b in blocks]
    rows = whole[0] if len(whole) == 1 else jnp.concatenate(whole, axis=0)
    x = rows[:, :width]
    scale = jnp.sum(rows[:, width:].astype(jnp.float32) * select_ref[...], axis=1, keepdims=True)
    w_gate = jnp.concatenate([wg0[...], wg1[...]], axis=0)
    w_up = jnp.concatenate([wu0[...], wu1[...]], axis=0)
    w_down = jnp.concatenate([wd0[...], wd1[...]], axis=0)
    contract = (((1,), (1,)), ((), ()))
    gate = lax.dot_general(x, w_gate, contract, preferred_element_type=jnp.float32)
    up = lax.dot_general(x, w_up, contract, preferred_element_type=jnp.float32)
    hidden = (gate / (1.0 + jnp.exp(-gate)) * up).astype(jnp.bfloat16)
    total = jnp.dot(hidden, w_down, preferred_element_type=jnp.float32)
    scaled = (total * scale).astype(jnp.bfloat16)
    start = 0
    for count, out in zip(counts, outs):
        out[...] = scaled[start : start + count]
        start += count


def run_expert(blocks, select, weights):
    counts = tuple(b.shape[0] for b in blocks)
    width = weights[0].shape[1]
    units = sum(w.shape[0] for w in weights)
    spec = pl.BlockSpec(memory_space=pltpu.VMEM)
    return pl.pallas_call(
        functools.partial(expert_kernel, counts),
        out_shape=[jax.ShapeDtypeStruct((c, width), jnp.bfloat16) for c in counts],
        in_specs=[spec] * (1 + len(blocks) + len(weights)),
        out_specs=[spec] * len(blocks),
        compiler_params=pltpu.CompilerParams(vmem_limit_bytes=VMEM_LIMIT),
        cost_estimate=pl.CostEstimate(
            flops=2 * sum(counts) * units * width,
            bytes_accessed=2 * units * width,
            transcendentals=sum(counts) * units // 3,
        ),
    )(select, *blocks, *weights)


def spread_kernel(n, head_ref, tokens_ref, ids_ref, scores_ref, mine_ref, lanes_ref):
    part = mine_ref.shape[0]
    first = head_ref[0] == 0
    mine_ref[...] = jnp.where(first, tokens_ref[:part], tokens_ref[part:])
    ids = jnp.where(first, ids_ref[:part], ids_ref[part:])
    scores = jnp.where(first, scores_ref[:part], scores_ref[part:])
    lane = lax.broadcasted_iota(jnp.int32, (part, LANES), 1)
    expert = lane % n
    dense = jnp.zeros((part, LANES), jnp.float32)
    for k in range(ids.shape[1]):
        dense = dense + jnp.where(expert == ids[:, k : k + 1], scores[:, k : k + 1], 0.0)
    packed = jnp.zeros((part, LANES), jnp.float32)
    for p in range(PIECES):
        piece = dense.astype(jnp.bfloat16).astype(jnp.float32)
        packed = jnp.where((lane >= p * n) & (lane < (p + 1) * n), piece, packed)
        dense = dense - piece
    lanes_ref[...] = packed.astype(jnp.bfloat16)


def spread(head, tokens, expert_ids, gate_scores):
    rows, half_width = tokens.shape
    spec = pl.BlockSpec(memory_space=pltpu.VMEM)
    return pl.pallas_call(
        functools.partial(spread_kernel, lax.axis_size("wide")),
        out_shape=[
            jax.ShapeDtypeStruct((rows // 2, half_width), jnp.bfloat16),
            jax.ShapeDtypeStruct((rows // 2, LANES), jnp.bfloat16),
        ],
        in_specs=[pl.BlockSpec(memory_space=pltpu.SMEM)] + [spec] * 3,
        out_specs=[spec] * 2,
        compiler_params=pltpu.CompilerParams(vmem_limit_bytes=VMEM_LIMIT),
        cost_estimate=pl.CostEstimate(
            flops=0, bytes_accessed=3 * rows * half_width, transcendentals=0
        ),
    )(head.reshape(1), tokens, expert_ids, gate_scores)


def join_kernel(head_ref, mine_ref, got_ref, lanes_ref, out_ref):
    part, half_width = mine_ref.shape
    first = head_ref[0] == 0
    mine = mine_ref[...]
    out_ref[:, :half_width] = jnp.where(first, mine, got_ref[part:])
    out_ref[:, half_width : 2 * half_width] = jnp.where(first, got_ref[:part], mine)
    out_ref[:, 2 * half_width :] = lanes_ref[...]


def join(head, mine, got, lanes):
    part, half_width = mine.shape
    spec = pl.BlockSpec(memory_space=pltpu.VMEM)
    return pl.pallas_call(
        join_kernel,
        out_shape=jax.ShapeDtypeStruct((part, 2 * half_width + LANES), jnp.bfloat16),
        in_specs=[pl.BlockSpec(memory_space=pltpu.SMEM)] + [spec] * 3,
        out_specs=spec,
        compiler_params=pltpu.CompilerParams(vmem_limit_bytes=VMEM_LIMIT),
        cost_estimate=pl.CostEstimate(
            flops=0, bytes_accessed=8 * part * half_width, transcendentals=0
        ),
    )(head.reshape(1), mine, got, lanes)


def fetch_kernel(count, *refs):
    copies = [
        pltpu.make_async_copy(refs[i], refs[count + i], refs[2 * count].at[i]) for i in range(count)
    ]
    for copy in copies:
        copy.start()
    for copy in copies:
        copy.wait()


def fetch(arrays):
    count = len(arrays)
    return pl.pallas_call(
        functools.partial(fetch_kernel, count),
        out_shape=[jax.ShapeDtypeStruct(a.shape, a.dtype) for a in arrays],
        in_specs=[pl.BlockSpec(memory_space=pltpu.HBM)] * count,
        out_specs=[pl.BlockSpec(memory_space=pltpu.VMEM)] * count,
        scratch_shapes=[pltpu.SemaphoreType.DMA((count,))],
        compiler_params=pltpu.CompilerParams(vmem_limit_bytes=VMEM_LIMIT),
        cost_estimate=pl.CostEstimate(
            flops=0, bytes_accessed=4 * sum(a.size for a in arrays), transcendentals=0
        ),
    )(*arrays)


def dense_local(tokens, expert_ids, gate_scores, gate_proj, up_proj, down_proj):
    n = lax.axis_size("wide")
    head = lax.axis_index("head")
    expert = lax.axis_index("wide")
    tok_rows, half_width = tokens.shape
    part = tok_rows // 2
    swap = ((0, 1), (1, 0))
    order = list(range(0, n, 2)) + list(range(n - 1, 0, -2))
    ahead = [(order[i], order[(i + 1) % n]) for i in range(n)]
    behind = [(b, a) for a, b in ahead]

    def forth(v):
        return lax.ppermute(v, "wide", ahead)

    def back(v):
        return lax.ppermute(v, "wide", behind)

    first = head == 0
    got = lax.ppermute(tokens, "head", swap)
    mine, lanes = spread(head, tokens, expert_ids, gate_scores)
    own = join(head, mine, got, lanes)
    lane = jnp.arange(LANES, dtype=jnp.int32)
    select = jnp.where(lane % n == expert, 1.0, 0.0).astype(jnp.float32)[None, :]

    own, *held = lax.optimization_barrier((own, gate_proj[0], up_proj[0], down_proj[0]))
    came = [lax.ppermute(w, "head", swap) for w in held]
    kept = fetch(held)

    reach = n // 2
    cut = part // 2
    near = {0: own}
    f = b = own
    sums = {}
    for k in range(1, reach):
        f, b = forth(f), back(b)
        if k == 1:
            f, b, *kept = lax.optimization_barrier((f, b, *kept))
        near[-k], near[k] = f, b
    weights = [w for pair in zip(kept, came) for w in pair]
    keys = sorted(i for i in near if abs(i) < reach - 1)
    done = run_expert([near[i] for i in keys], select, weights)
    f, b, *done = lax.optimization_barrier((f, b, *done))
    sums.update(zip(keys, done))
    keys = [1 - reach, reach - 1]
    done = run_expert([f, b], select, weights)
    f, b = forth(f[:cut]), back(b[cut:])
    f, b, *done = lax.optimization_barrier((f, b, *done))
    sums.update(zip(keys, done))
    far = run_expert([f, b], select, weights)

    f, b = forth(far[0]), back(far[1])
    for k in range(reach - 1, 0, -1):
        up_sum = sums[k].astype(jnp.float32)
        down_sum = sums[-k].astype(jnp.float32)
        if k == reach - 1:
            up_sum = jnp.concatenate([up_sum[:cut] + f.astype(jnp.float32), up_sum[cut:]], axis=0)
            down_sum = jnp.concatenate(
                [down_sum[:cut], down_sum[cut:] + b.astype(jnp.float32)], axis=0
            )
        else:
            up_sum = up_sum + f.astype(jnp.float32)
            down_sum = down_sum + b.astype(jnp.float32)
        f, b = forth(up_sum.astype(jnp.bfloat16)), back(down_sum.astype(jnp.bfloat16))
    mixed = (sums[0].astype(jnp.float32) + f.astype(jnp.float32) + b.astype(jnp.float32)).astype(
        jnp.bfloat16
    )
    left, right = mixed[:, :half_width], mixed[:, half_width:]
    keep = jnp.where(first, left, right)
    rest = lax.ppermute(jnp.where(first, right, left), "head", swap)
    return jnp.concatenate(
        [jnp.where(first, keep, rest), jnp.where(first, rest, keep)], axis=0
    )


def local(tokens, expert_ids, gate_scores, gate_proj, up_proj, down_proj):
    n = lax.axis_size("wide")
    dense = expert_ids.shape[1] == n and lax.axis_size("head") == 2 and n % 2 == 0
    if dense and tokens.shape[0] % 64 == 0 and PIECES * n <= LANES:
        return dense_local(tokens, expert_ids, gate_scores, gate_proj, up_proj, down_proj)
    return sparse_local(tokens, expert_ids, gate_scores, gate_proj, up_proj, down_proj)


def solution(mesh):
    return jax.shard_map(
        local,
        mesh=mesh,
        in_specs=(
            P(("groups", "wide"), "head"),
            P(("groups", "wide"), None),
            P(("groups", "wide"), None),
            P("wide", "head", None),
            P("wide", "head", None),
            P("wide", "head", None),
        ),
        out_specs=P(("groups", "wide"), "head"),
        check_vma=False,
    )
```

```python
import functools

import jax
import jax.numpy as jnp
from jax import lax
from jax.experimental import pallas as pl
from jax.experimental.pallas import tpu as pltpu
from jax.sharding import PartitionSpec as P

LANES = 128
PIECES = 3
VMEM_LIMIT = 16 * 2**20
SMALL_LIMIT = 4 * 2**20
MARK = (8, 128)


def sparse_local(tokens, expert_ids, gate_scores, gate_proj, up_proj, down_proj):
    experts = lax.axis_size("wide")
    tok_rows, top_count = expert_ids.shape
    ceiling = (tok_rows * top_count + experts - 1) // experts
    capacity = min(tok_rows, max(2, tok_rows // 8, 2 * ceiling))
    flat_ids = expert_ids.reshape(-1)
    expert_numbers = jnp.arange(experts, dtype=jnp.int32)
    onehot = (flat_ids[:, None] == expert_numbers[None, :]).astype(jnp.int32)
    earlier = jnp.cumsum(onehot, axis=0) - onehot
    slot_index = jnp.sum(earlier * onehot, axis=1)
    position = flat_ids * capacity + slot_index
    targets = jnp.arange(experts * capacity, dtype=jnp.int32)
    placing = jnp.any(
        position.reshape(tok_rows, top_count)[:, :, None] == targets[None, None, :], axis=1
    ).astype(jnp.bfloat16)
    w_gate = gate_proj[0]
    w_up = up_proj[0]
    w_down = down_proj[0]
    placed = lax.dot_general(
        placing, tokens, (((0,), (0,)), ((), ())), preferred_element_type=jnp.float32
    )
    outgoing = placed.astype(jnp.bfloat16).reshape(experts, capacity, tokens.shape[1])
    full_rows = lax.all_gather(
        lax.all_to_all(outgoing, "wide", split_axis=0, concat_axis=0, tiled=True),
        "head",
        axis=2,
        tiled=True,
    )
    src_count, item_count, feature_width = full_rows.shape
    stacked = full_rows.reshape(src_count * item_count, feature_width)
    gate_part = lax.dot_general(
        stacked, w_gate, (((1,), (1,)), ((), ())), preferred_element_type=jnp.float32
    )
    up_part = lax.dot_general(
        stacked, w_up, (((1,), (1,)), ((), ())), preferred_element_type=jnp.float32
    )
    hidden = (jax.nn.silu(gate_part) * up_part).astype(jnp.bfloat16)
    partial_value = jnp.dot(hidden, w_down, preferred_element_type=jnp.float32)
    partial_value = partial_value.reshape(src_count, item_count, feature_width)
    back = lax.psum_scatter(
        partial_value.astype(jnp.bfloat16), "head", scatter_dimension=2, tiled=True
    ).astype(jnp.float32)
    returned = lax.all_to_all(
        back.astype(jnp.bfloat16), "wide", split_axis=0, concat_axis=0, tiled=True
    ).astype(back.dtype)
    picked = returned.reshape(experts * capacity, returned.shape[2])[position]
    picked = picked.reshape(tok_rows, top_count, returned.shape[2])
    mixed = jnp.sum(gate_scores[:, :, None] * picked, axis=1)
    return mixed.astype(jnp.bfloat16)


def in_vmem():
    return pl.BlockSpec(memory_space=pltpu.VMEM)


def in_hbm():
    return pl.BlockSpec(memory_space=pltpu.HBM)


def hbm(v):
    return pltpu.with_memory_space_constraint(v, pltpu.HBM)


def spread_kernel(n, head_ref, tokens_hbm, ids_hbm, scores_hbm, mine_ref, lanes_ref, ids, scores, sems):
    part = mine_ref.shape[0]
    head = head_ref[0]
    copies = [
        pltpu.make_async_copy(ids_hbm, ids, sems.at[0]),
        pltpu.make_async_copy(scores_hbm, scores, sems.at[1]),
        pltpu.make_async_copy(
            tokens_hbm.at[pl.ds(pl.multiple_of(head * part, part), part)], mine_ref, sems.at[2]
        ),
    ]
    for copy in copies:
        copy.start()
    copies[0].wait()
    copies[1].wait()
    names, values = ids[...], scores[...]
    top, rows = names.shape
    expert = lax.broadcasted_iota(jnp.int32, (n, rows), 0)
    dense = jnp.zeros((n, rows), jnp.float32)
    for k in range(top):
        dense = dense + jnp.where(expert == names[k : k + 1], values[k : k + 1], 0.0)
    pieces = []
    for _ in range(PIECES):
        piece = dense.astype(jnp.bfloat16).astype(jnp.float32)
        pieces.append(piece)
        dense = dense - piece
    pieces.append(jnp.zeros((LANES - PIECES * n, rows), jnp.float32))
    packed = jnp.concatenate(pieces, axis=0).T
    lanes_ref[...] = jnp.where(head == 0, packed[:part], packed[part:]).astype(jnp.bfloat16)
    copies[2].wait()


def spread(head, tokens, expert_ids, gate_scores):
    rows, half_width = tokens.shape
    n = lax.axis_size("wide")
    top = expert_ids.shape[1]
    return pl.pallas_call(
        functools.partial(spread_kernel, n),
        out_shape=[
            jax.ShapeDtypeStruct((rows // 2, half_width), jnp.bfloat16),
            jax.ShapeDtypeStruct((rows // 2, LANES), jnp.bfloat16),
        ],
        in_specs=[pl.BlockSpec(memory_space=pltpu.SMEM)] + [in_hbm()] * 3,
        out_specs=[in_vmem()] * 2,
        scratch_shapes=[
            pltpu.VMEM((top, rows), jnp.int32),
            pltpu.VMEM((top, rows), jnp.float32),
            pltpu.SemaphoreType.DMA((3,)),
        ],
        compiler_params=pltpu.CompilerParams(vmem_limit_bytes=SMALL_LIMIT),
        cost_estimate=pl.CostEstimate(
            flops=0, bytes_accessed=3 * rows * half_width, transcendentals=0
        ),
    )(head.reshape(1), hbm(tokens), hbm(expert_ids.T), hbm(gate_scores.T))


def join_kernel(head_ref, mine_ref, got_ref, lanes_ref, out_ref):
    part, half_width = mine_ref.shape
    first = head_ref[0] == 0
    mine = mine_ref[...]
    out_ref[:, :half_width] = jnp.where(first, mine, got_ref[part:])
    out_ref[:, half_width : 2 * half_width] = jnp.where(first, got_ref[:part], mine)
    out_ref[:, 2 * half_width :] = lanes_ref[...]


def join(head, mine, got, lanes):
    part, half_width = mine.shape
    return pl.pallas_call(
        join_kernel,
        out_shape=jax.ShapeDtypeStruct((part, 2 * half_width + LANES), jnp.bfloat16),
        in_specs=[pl.BlockSpec(memory_space=pltpu.SMEM)] + [in_vmem()] * 3,
        out_specs=in_vmem(),
        compiler_params=pltpu.CompilerParams(vmem_limit_bytes=SMALL_LIMIT),
        cost_estimate=pl.CostEstimate(
            flops=0, bytes_accessed=8 * part * half_width, transcendentals=0
        ),
    )(head.reshape(1), mine, got, lanes)


def gather_kernel(count, *refs):
    kept, came = refs[:count], refs[count : 2 * count]
    outs, mark, sems = refs[2 * count : 3 * count], refs[3 * count], refs[3 * count + 1]
    copies = []
    for i in range(count):
        units = kept[i].shape[0]
        cut = units // 2
        for j, (source, target) in enumerate(
            (
                (kept[i].at[:cut], outs[i].at[:cut]),
                (kept[i].at[cut:], outs[i].at[cut:units]),
                (came[i], outs[i].at[units:]),
            )
        ):
            copies.append(pltpu.make_async_copy(source, target, sems.at[i, j]))
    for copy in copies:
        copy.start()
    mark[...] = jnp.zeros(mark.shape, mark.dtype)
    for copy in copies:
        copy.wait()


def gather_weights(kept, came):
    count = len(kept)
    units, width = kept[0].shape
    *whole, mark = pl.pallas_call(
        functools.partial(gather_kernel, count),
        out_shape=[jax.ShapeDtypeStruct((2 * units, width), jnp.bfloat16)] * count
        + [jax.ShapeDtypeStruct(MARK, jnp.float32)],
        in_specs=[in_hbm()] * count + [pl.BlockSpec(memory_space=pl.ANY)] * count,
        out_specs=[in_vmem()] * (count + 1),
        scratch_shapes=[pltpu.SemaphoreType.DMA((count, 3))],
        compiler_params=pltpu.CompilerParams(vmem_limit_bytes=SMALL_LIMIT),
        cost_estimate=pl.CostEstimate(
            flops=0, bytes_accessed=4 * count * units * width, transcendentals=0
        ),
    )(*[hbm(w) for w in kept], *came)
    return whole, mark


def expert_kernel(counts, _, select_ref, *refs):
    blocks = refs[: len(counts)]
    wg, wu, wd = refs[len(counts) : len(counts) + 3]
    outs = refs[len(counts) + 3 : -1]
    mark = refs[-1]
    width = wg.shape[1]
    whole = [b[...] for b in blocks]
    rows = whole[0] if len(whole) == 1 else jnp.concatenate(whole, axis=0)
    x = rows[:, :width]
    scale = jnp.sum(rows[:, width:].astype(jnp.float32) * select_ref[...], axis=1, keepdims=True)
    contract = (((1,), (1,)), ((), ()))
    gate = lax.dot_general(x, wg[...], contract, preferred_element_type=jnp.float32)
    up = lax.dot_general(x, wu[...], contract, preferred_element_type=jnp.float32)
    hidden = (gate / (1.0 + jnp.exp(-gate)) * up).astype(jnp.bfloat16)
    total = jnp.dot(hidden, wd[...], preferred_element_type=jnp.float32)
    scaled = (total * scale).astype(jnp.bfloat16)
    start = 0
    for count, out in zip(counts, outs):
        out[...] = scaled[start : start + count]
        start += count
    mark[...] = jnp.zeros(mark.shape, mark.dtype)


def run_expert(mark, blocks, select, weights):
    counts = tuple(b.shape[0] for b in blocks)
    units, width = weights[0].shape
    *outs, mark = pl.pallas_call(
        functools.partial(expert_kernel, counts),
        out_shape=[jax.ShapeDtypeStruct((c, width), jnp.bfloat16) for c in counts]
        + [jax.ShapeDtypeStruct(MARK, jnp.float32)],
        in_specs=[pl.BlockSpec(memory_space=pl.ANY)]
        + [in_vmem()] * (1 + len(blocks) + len(weights)),
        out_specs=[in_vmem()] * (len(blocks) + 1),
        compiler_params=pltpu.CompilerParams(vmem_limit_bytes=VMEM_LIMIT),
        cost_estimate=pl.CostEstimate(
            flops=6 * sum(counts) * units * width,
            bytes_accessed=6 * units * width,
            transcendentals=sum(counts) * units,
        ),
    )(mark, select, *blocks, *weights)
    return outs, mark


def after(mark, *values):
    return lax.optimization_barrier((mark, *values))


def dense_local(tokens, expert_ids, gate_scores, gate_proj, up_proj, down_proj):
    n = lax.axis_size("wide")
    head = lax.axis_index("head")
    expert = lax.axis_index("wide")
    tok_rows, half_width = tokens.shape
    part = tok_rows // 2
    swap = ((0, 1), (1, 0))
    order = list(range(0, n, 2)) + list(range(n - 1, 0, -2))
    ahead = [(order[i], order[(i + 1) % n]) for i in range(n)]
    behind = [(b, a) for a, b in ahead]

    def forth(v):
        return lax.ppermute(v, "wide", ahead)

    def back(v):
        return lax.ppermute(v, "wide", behind)

    first = head == 0
    got = lax.ppermute(tokens, "head", swap)
    mine, lanes = spread(head, tokens, expert_ids, gate_scores)
    kept = (gate_proj[0], up_proj[0], down_proj[0])
    got, *kept = after(got, *kept)
    came = [lax.ppermute(w, "head", swap) for w in kept]
    own = join(head, mine, got, lanes)
    lane = jnp.arange(LANES, dtype=jnp.int32)
    select = jnp.where(lane % n == expert, 1.0, 0.0).astype(jnp.float32)[None, :]

    reach = n // 2
    cut = part // 2
    near = {0: own}
    f, b = forth(own), back(own)
    near[-1], near[1] = f, b
    weights, mark = gather_weights(kept, came)
    for k in range(2, reach):
        f, b = forth(f), back(b)
        near[-k], near[k] = f, b
        if k == 2:
            mark, f, b = after(mark, f, b)
    sums = {}
    keys = sorted(i for i in near if abs(i) < reach - 1)
    done, mark = run_expert(mark, [near[i] for i in keys], select, weights)
    sums.update(zip(keys, done))
    mark, f, b = after(mark, f, b)
    f, b = forth(f[:cut]), back(b[cut:])
    keys = [1 - reach, reach - 1]
    done, mark = run_expert(mark, [near[i] for i in keys], select, weights)
    sums.update(zip(keys, done))
    mark, f, b = after(mark, f, b)
    far, _ = run_expert(mark, [f, b], select, weights)

    f, b = forth(far[0]), back(far[1])
    for k in range(reach - 1, 0, -1):
        up_sum = sums[k].astype(jnp.float32)
        down_sum = sums[-k].astype(jnp.float32)
        if k == reach - 1:
            up_sum = jnp.concatenate([up_sum[:cut] + f.astype(jnp.float32), up_sum[cut:]], axis=0)
            down_sum = jnp.concatenate(
                [down_sum[:cut], down_sum[cut:] + b.astype(jnp.float32)], axis=0
            )
        else:
            up_sum = up_sum + f.astype(jnp.float32)
            down_sum = down_sum + b.astype(jnp.float32)
        f, b = forth(up_sum.astype(jnp.bfloat16)), back(down_sum.astype(jnp.bfloat16))
    mixed = (sums[0].astype(jnp.float32) + f.astype(jnp.float32) + b.astype(jnp.float32)).astype(
        jnp.bfloat16
    )
    left, right = mixed[:, :half_width], mixed[:, half_width:]
    keep = jnp.where(first, left, right)
    rest = lax.ppermute(jnp.where(first, right, left), "head", swap)
    return jnp.concatenate(
        [jnp.where(first, keep, rest), jnp.where(first, rest, keep)], axis=0
    )


def local(tokens, expert_ids, gate_scores, gate_proj, up_proj, down_proj):
    n = lax.axis_size("wide")
    dense = expert_ids.shape[1] == n and lax.axis_size("head") == 2 and n % 2 == 0
    if dense and tokens.shape[0] % 64 == 0 and PIECES * n <= LANES:
        return dense_local(tokens, expert_ids, gate_scores, gate_proj, up_proj, down_proj)
    return sparse_local(tokens, expert_ids, gate_scores, gate_proj, up_proj, down_proj)


def solution(mesh):
    return jax.shard_map(
        local,
        mesh=mesh,
        in_specs=(
            P(("groups", "wide"), "head"),
            P(("groups", "wide"), None),
            P(("groups", "wide"), None),
            P("wide", "head", None),
            P("wide", "head", None),
            P("wide", "head", None),
        ),
        out_specs=P(("groups", "wide"), "head"),
        check_vma=False,
    )
```

```python
import functools

import jax
import jax.numpy as jnp
from jax import lax
from jax.experimental import pallas as pl
from jax.experimental.pallas import tpu as pltpu
from jax.sharding import PartitionSpec as P

LANES = 128
PIECES = 3
VMEM_LIMIT = 16 * 2**20
SMALL_LIMIT = 1 * 2**20
MARK = (8, 128)


def cost(size):
    return pl.CostEstimate(flops=0, bytes_accessed=size, transcendentals=0)


NO_COST = cost(1)
GATHER_COST = 1
TOUCH_COST = 1
EXPERT_COST = 1
ADD_COST = 1


def sparse_local(tokens, expert_ids, gate_scores, gate_proj, up_proj, down_proj):
    experts = lax.axis_size("wide")
    tok_rows, top_count = expert_ids.shape
    ceiling = (tok_rows * top_count + experts - 1) // experts
    capacity = min(tok_rows, max(2, tok_rows // 8, 2 * ceiling))
    flat_ids = expert_ids.reshape(-1)
    expert_numbers = jnp.arange(experts, dtype=jnp.int32)
    onehot = (flat_ids[:, None] == expert_numbers[None, :]).astype(jnp.int32)
    earlier = jnp.cumsum(onehot, axis=0) - onehot
    slot_index = jnp.sum(earlier * onehot, axis=1)
    position = flat_ids * capacity + slot_index
    targets = jnp.arange(experts * capacity, dtype=jnp.int32)
    placing = jnp.any(
        position.reshape(tok_rows, top_count)[:, :, None] == targets[None, None, :], axis=1
    ).astype(jnp.bfloat16)
    w_gate = gate_proj[0]
    w_up = up_proj[0]
    w_down = down_proj[0]
    placed = lax.dot_general(
        placing, tokens, (((0,), (0,)), ((), ())), preferred_element_type=jnp.float32
    )
    outgoing = placed.astype(jnp.bfloat16).reshape(experts, capacity, tokens.shape[1])
    full_rows = lax.all_gather(
        lax.all_to_all(outgoing, "wide", split_axis=0, concat_axis=0, tiled=True),
        "head",
        axis=2,
        tiled=True,
    )
    src_count, item_count, feature_width = full_rows.shape
    stacked = full_rows.reshape(src_count * item_count, feature_width)
    gate_part = lax.dot_general(
        stacked, w_gate, (((1,), (1,)), ((), ())), preferred_element_type=jnp.float32
    )
    up_part = lax.dot_general(
        stacked, w_up, (((1,), (1,)), ((), ())), preferred_element_type=jnp.float32
    )
    hidden = (jax.nn.silu(gate_part) * up_part).astype(jnp.bfloat16)
    partial_value = jnp.dot(hidden, w_down, preferred_element_type=jnp.float32)
    partial_value = partial_value.reshape(src_count, item_count, feature_width)
    back = lax.psum_scatter(
        partial_value.astype(jnp.bfloat16), "head", scatter_dimension=2, tiled=True
    ).astype(jnp.float32)
    returned = lax.all_to_all(
        back.astype(jnp.bfloat16), "wide", split_axis=0, concat_axis=0, tiled=True
    ).astype(back.dtype)
    picked = returned.reshape(experts * capacity, returned.shape[2])[position]
    picked = picked.reshape(tok_rows, top_count, returned.shape[2])
    mixed = jnp.sum(gate_scores[:, :, None] * picked, axis=1)
    return mixed.astype(jnp.bfloat16)


def in_vmem():
    return pl.BlockSpec(memory_space=pltpu.VMEM)


def in_hbm():
    return pl.BlockSpec(memory_space=pltpu.HBM)


def hbm(v):
    return pltpu.with_memory_space_constraint(v, pltpu.HBM)


def spread_kernel(n, head_ref, tokens_hbm, ids_hbm, scores_hbm, mine_ref, lanes_ref, ids, scores, sems):
    part = mine_ref.shape[0]
    head = head_ref[0]
    copies = [
        pltpu.make_async_copy(ids_hbm, ids, sems.at[0]),
        pltpu.make_async_copy(scores_hbm, scores, sems.at[1]),
        pltpu.make_async_copy(
            tokens_hbm.at[pl.ds(pl.multiple_of(head * part, part), part)], mine_ref, sems.at[2]
        ),
    ]
    for copy in copies:
        copy.start()
    copies[0].wait()
    copies[1].wait()
    names, values = ids[...], scores[...]
    top, rows = names.shape
    expert = lax.broadcasted_iota(jnp.int32, (n, rows), 0)
    dense = jnp.zeros((n, rows), jnp.float32)
    for k in range(top):
        dense = dense + jnp.where(expert == names[k : k + 1], values[k : k + 1], 0.0)
    pieces = []
    for _ in range(PIECES):
        piece = dense.astype(jnp.bfloat16).astype(jnp.float32)
        pieces.append(piece)
        dense = dense - piece
    pieces.append(jnp.zeros((LANES - PIECES * n, rows), jnp.float32))
    packed = jnp.concatenate(pieces, axis=0).T
    lanes_ref[...] = jnp.where(head == 0, packed[:part], packed[part:]).astype(jnp.bfloat16)
    copies[2].wait()


def spread(head, tokens, expert_ids, gate_scores):
    rows, half_width = tokens.shape
    n = lax.axis_size("wide")
    top = expert_ids.shape[1]
    return pl.pallas_call(
        functools.partial(spread_kernel, n),
        out_shape=[
            jax.ShapeDtypeStruct((rows // 2, half_width), jnp.bfloat16),
            jax.ShapeDtypeStruct((rows // 2, LANES), jnp.bfloat16),
        ],
        in_specs=[pl.BlockSpec(memory_space=pltpu.SMEM)] + [in_hbm()] * 3,
        out_specs=[in_vmem()] * 2,
        scratch_shapes=[
            pltpu.VMEM((top, rows), jnp.int32),
            pltpu.VMEM((top, rows), jnp.float32),
            pltpu.SemaphoreType.DMA((3,)),
        ],
        compiler_params=pltpu.CompilerParams(vmem_limit_bytes=SMALL_LIMIT),
        cost_estimate=NO_COST,
    )(head.reshape(1), hbm(tokens), hbm(expert_ids.T), hbm(gate_scores.T))


def join_kernel(head_ref, mine_ref, got_ref, lanes_ref, out_ref):
    part, half_width = mine_ref.shape
    first = head_ref[0] == 0
    mine = mine_ref[...]
    out_ref[:, :half_width] = jnp.where(first, mine, got_ref[part:])
    out_ref[:, half_width : 2 * half_width] = jnp.where(first, got_ref[:part], mine)
    out_ref[:, 2 * half_width :] = lanes_ref[...]


def join(head, mine, got, lanes):
    part, half_width = mine.shape
    return pl.pallas_call(
        join_kernel,
        out_shape=jax.ShapeDtypeStruct((part, 2 * half_width + LANES), jnp.bfloat16),
        in_specs=[pl.BlockSpec(memory_space=pltpu.SMEM)] + [in_vmem()] * 3,
        out_specs=in_vmem(),
        compiler_params=pltpu.CompilerParams(vmem_limit_bytes=SMALL_LIMIT),
        cost_estimate=NO_COST,
    )(head.reshape(1), mine, got, lanes)


def gather_kernel(count, _, *refs):
    kept, came = refs[:count], refs[count : 2 * count]
    outs, mark, sems = refs[2 * count : 3 * count], refs[3 * count], refs[3 * count + 1]
    copies = []
    for i in range(count):
        units = kept[i].shape[0]
        cut = units // 2
        for j, (source, target) in enumerate(
            (
                (kept[i].at[:cut], outs[i].at[:cut]),
                (kept[i].at[cut:], outs[i].at[cut:units]),
                (came[i], outs[i].at[units:]),
            )
        ):
            copies.append(pltpu.make_async_copy(source, target, sems.at[i, j]))
    for copy in copies:
        copy.start()
    mark[...] = jnp.zeros(mark.shape, mark.dtype)
    for copy in copies:
        copy.wait()


def gather_weights(mark, kept, came):
    count = len(kept)
    units, width = kept[0].shape
    *whole, mark = pl.pallas_call(
        functools.partial(gather_kernel, count),
        out_shape=[jax.ShapeDtypeStruct((2 * units, width), jnp.bfloat16)] * count
        + [jax.ShapeDtypeStruct(MARK, jnp.float32)],
        in_specs=[pl.BlockSpec(memory_space=pl.ANY)]
        + [in_hbm()] * count
        + [pl.BlockSpec(memory_space=pl.ANY)] * count,
        out_specs=[in_vmem()] * (count + 1),
        scratch_shapes=[pltpu.SemaphoreType.DMA((count, 3))],
        compiler_params=pltpu.CompilerParams(vmem_limit_bytes=SMALL_LIMIT),
        cost_estimate=cost(GATHER_COST),
    )(mark, *[hbm(w) for w in kept], *came)
    return whole, mark


def touch_kernel(*refs):
    refs[-1][...] = jnp.zeros(refs[-1].shape, refs[-1].dtype)


def touch(*values):
    return pl.pallas_call(
        touch_kernel,
        out_shape=jax.ShapeDtypeStruct(MARK, jnp.float32),
        in_specs=[pl.BlockSpec(memory_space=pl.ANY)] * len(values),
        out_specs=in_vmem(),
        compiler_params=pltpu.CompilerParams(vmem_limit_bytes=SMALL_LIMIT),
        cost_estimate=cost(TOUCH_COST),
    )(*values)


def expert_kernel(count, _, select_ref, *refs):
    blocks = refs[:count]
    wg, wu, wd = refs[count : count + 3]
    outs = refs[count + 3 : -1]
    mark = refs[-1]
    width = wg.shape[1]
    whole = [b[...] for b in blocks]
    rows = whole[0] if len(whole) == 1 else jnp.concatenate(whole, axis=0)
    x = rows[:, :width]
    scale = jnp.sum(rows[:, width:].astype(jnp.float32) * select_ref[...], axis=1, keepdims=True)
    contract = (((1,), (1,)), ((), ()))
    gate = lax.dot_general(x, wg[...], contract, preferred_element_type=jnp.float32)
    up = lax.dot_general(x, wu[...], contract, preferred_element_type=jnp.float32)
    hidden = (gate / (1.0 + jnp.exp(-gate)) * up).astype(jnp.bfloat16)
    total = jnp.dot(hidden, wd[...], preferred_element_type=jnp.float32)
    scaled = (total * scale).astype(jnp.bfloat16)
    start = 0
    for out in outs:
        out[...] = scaled[start : start + out.shape[0]]
        start += out.shape[0]
    mark[...] = jnp.zeros(mark.shape, mark.dtype)


def run_expert(mark, groups, select, weights):
    blocks = [b for group in groups for b in group]
    counts = [sum(b.shape[0] for b in group) for group in groups]
    units, width = weights[0].shape
    *outs, mark = pl.pallas_call(
        functools.partial(expert_kernel, len(blocks)),
        out_shape=[jax.ShapeDtypeStruct((c, width), jnp.bfloat16) for c in counts]
        + [jax.ShapeDtypeStruct(MARK, jnp.float32)],
        in_specs=[pl.BlockSpec(memory_space=pl.ANY)]
        + [in_vmem()] * (1 + len(blocks) + len(weights)),
        out_specs=[in_vmem()] * (len(groups) + 1),
        compiler_params=pltpu.CompilerParams(vmem_limit_bytes=VMEM_LIMIT),
        cost_estimate=cost(EXPERT_COST),
    )(mark, select, *blocks, *weights)
    return outs, mark


def add_kernel(_, a_ref, b_ref, out_ref, mark):
    out_ref[...] = (a_ref[...].astype(jnp.float32) + b_ref[...].astype(jnp.float32)).astype(
        jnp.bfloat16
    )
    mark[...] = jnp.zeros(mark.shape, mark.dtype)


def add_rows(mark, a, b):
    return pl.pallas_call(
        add_kernel,
        out_shape=[
            jax.ShapeDtypeStruct(a.shape, jnp.bfloat16),
            jax.ShapeDtypeStruct(MARK, jnp.float32),
        ],
        in_specs=[pl.BlockSpec(memory_space=pl.ANY)] + [in_vmem()] * 2,
        out_specs=[in_vmem()] * 2,
        compiler_params=pltpu.CompilerParams(vmem_limit_bytes=SMALL_LIMIT),
        cost_estimate=cost(ADD_COST),
    )(mark, a, b)


def after(mark, *values):
    return lax.optimization_barrier((mark, *values))


def dense_local(tokens, expert_ids, gate_scores, gate_proj, up_proj, down_proj):
    n = lax.axis_size("wide")
    head = lax.axis_index("head")
    expert = lax.axis_index("wide")
    tok_rows, half_width = tokens.shape
    part = tok_rows // 2
    swap = ((0, 1), (1, 0))

    def pair(v):
        return lax.ppermute(v, "wide", [(w, w ^ 1) for w in range(n)])

    def column(v, k):
        return lax.ppermute(v, "wide", [(w, w ^ (2 * k)) for w in range(n)])

    def add(*terms):
        return sum(t.astype(jnp.float32) for t in terms).astype(jnp.bfloat16)

    first = head == 0
    got = lax.ppermute(tokens, "head", swap)
    mine, lanes = spread(head, tokens, expert_ids, gate_scores)
    kept = (gate_proj[0], up_proj[0], down_proj[0])
    lanes, got = after(lanes, got)
    own = join(head, mine, got, lanes)
    lane = jnp.arange(LANES, dtype=jnp.int32)
    select = jnp.where(lane % n == expert, 1.0, 0.0).astype(jnp.float32)[None, :]

    last = 2
    mid = list(range(3, n // 2))
    got, *held = after(got, *kept)
    came = [lax.ppermute(w, "head", swap) for w in held]
    block = {0: own}
    block.update({k: column(own, k) for k in mid + [1]})
    over = {0: pair(own), 1: pair(block[1])}
    block[1], own_again = after(block[1], own)
    block[last] = column(own_again, last)
    mark = touch(block[1], *came[:2])
    for k in mid:
        mark, block[k] = after(mark, block[k])
        over[k] = pair(block[k])
    weights, mark = gather_weights(mark, kept, came)
    mark, block[last] = after(mark, block[last])
    over[last] = pair(block[last])

    groups = [[block[0]], [block[1]]] + [[v[k]] for k in mid for v in (block, over)]
    done, mark = run_expert(mark, groups + [[over[0], over[1]]], select, weights)
    here = {0: done[0], 1: done[1]}
    there = {}
    for i, k in enumerate(mid):
        here[k] = done[2 + 2 * i]
        there[k] = pair(done[3 + 2 * i])
    first_two = pair(done[-1])
    there[0], there[1] = first_two[:part], first_two[part:]
    done, mark = run_expert(mark, [[block[last]], [over[last]]], select, weights)
    here[last] = done[0]
    there[last] = pair(done[1])
    returned = []
    for k in mid + [1, last]:
        total, mark = add_rows(mark, here[k], there[k])
        returned.append(column(total, k))
    mixed = add(here[0], there[0], *returned)
    left, right = mixed[:, :half_width], mixed[:, half_width:]
    keep = jnp.where(first, left, right)
    rest = lax.ppermute(jnp.where(first, right, left), "head", swap)
    return jnp.concatenate(
        [jnp.where(first, keep, rest), jnp.where(first, rest, keep)], axis=0
    )


def local(tokens, expert_ids, gate_scores, gate_proj, up_proj, down_proj):
    n = lax.axis_size("wide")
    named = expert_ids.shape[1]
    dense = named == n and n >= 4 and n & (n - 1) == 0 and PIECES * n <= LANES
    if dense and lax.axis_size("head") == 2 and tokens.shape[0] % 32 == 0:
        return dense_local(tokens, expert_ids, gate_scores, gate_proj, up_proj, down_proj)
    return sparse_local(tokens, expert_ids, gate_scores, gate_proj, up_proj, down_proj)


def solution(mesh):
    return jax.shard_map(
        local,
        mesh=mesh,
        in_specs=(
            P(("groups", "wide"), "head"),
            P(("groups", "wide"), None),
            P(("groups", "wide"), None),
            P("wide", "head", None),
            P("wide", "head", None),
            P("wide", "head", None),
        ),
        out_specs=P(("groups", "wide"), "head"),
        check_vma=False,
    )
```

```python
import functools

import jax
import jax.numpy as jnp
from jax import lax
from jax.experimental import pallas as pl
from jax.experimental.pallas import tpu as pltpu
from jax.sharding import PartitionSpec as P

LANES = 128
PIECES = 3
VMEM_LIMIT = 16 * 2**20
SMALL_LIMIT = 2 * 2**20
MARK = (8, 128)


def cost(size):
    return pl.CostEstimate(flops=0, bytes_accessed=size, transcendentals=0)


NO_COST = cost(1)
GATHER_COST = 1
TOUCH_COST = 1000000
EXPERT_COST = 1
ADD_COST = 1000000


def sparse_local(tokens, expert_ids, gate_scores, gate_proj, up_proj, down_proj):
    experts = lax.axis_size("wide")
    tok_rows, top_count = expert_ids.shape
    ceiling = (tok_rows * top_count + experts - 1) // experts
    capacity = min(tok_rows, max(2, tok_rows // 8, 2 * ceiling))
    flat_ids = expert_ids.reshape(-1)
    expert_numbers = jnp.arange(experts, dtype=jnp.int32)
    onehot = (flat_ids[:, None] == expert_numbers[None, :]).astype(jnp.int32)
    earlier = jnp.cumsum(onehot, axis=0) - onehot
    slot_index = jnp.sum(earlier * onehot, axis=1)
    position = flat_ids * capacity + slot_index
    targets = jnp.arange(experts * capacity, dtype=jnp.int32)
    placing = jnp.any(
        position.reshape(tok_rows, top_count)[:, :, None] == targets[None, None, :], axis=1
    ).astype(jnp.bfloat16)
    w_gate = gate_proj[0]
    w_up = up_proj[0]
    w_down = down_proj[0]
    placed = lax.dot_general(
        placing, tokens, (((0,), (0,)), ((), ())), preferred_element_type=jnp.float32
    )
    outgoing = placed.astype(jnp.bfloat16).reshape(experts, capacity, tokens.shape[1])
    full_rows = lax.all_gather(
        lax.all_to_all(outgoing, "wide", split_axis=0, concat_axis=0, tiled=True),
        "head",
        axis=2,
        tiled=True,
    )
    src_count, item_count, feature_width = full_rows.shape
    stacked = full_rows.reshape(src_count * item_count, feature_width)
    gate_part = lax.dot_general(
        stacked, w_gate, (((1,), (1,)), ((), ())), preferred_element_type=jnp.float32
    )
    up_part = lax.dot_general(
        stacked, w_up, (((1,), (1,)), ((), ())), preferred_element_type=jnp.float32
    )
    hidden = (jax.nn.silu(gate_part) * up_part).astype(jnp.bfloat16)
    partial_value = jnp.dot(hidden, w_down, preferred_element_type=jnp.float32)
    partial_value = partial_value.reshape(src_count, item_count, feature_width)
    back = lax.psum_scatter(
        partial_value.astype(jnp.bfloat16), "head", scatter_dimension=2, tiled=True
    ).astype(jnp.float32)
    returned = lax.all_to_all(
        back.astype(jnp.bfloat16), "wide", split_axis=0, concat_axis=0, tiled=True
    ).astype(back.dtype)
    picked = returned.reshape(experts * capacity, returned.shape[2])[position]
    picked = picked.reshape(tok_rows, top_count, returned.shape[2])
    mixed = jnp.sum(gate_scores[:, :, None] * picked, axis=1)
    return mixed.astype(jnp.bfloat16)


def in_vmem():
    return pl.BlockSpec(memory_space=pltpu.VMEM)


def in_hbm():
    return pl.BlockSpec(memory_space=pltpu.HBM)


def hbm(v):
    return pltpu.with_memory_space_constraint(v, pltpu.HBM)


def spread_kernel(
    n, head_ref, expert_ref, tokens_hbm, ids_hbm, scores_hbm, mine_ref, lanes_ref, select_ref, ids, scores, sems
):
    part = mine_ref.shape[0]
    head = head_ref[0]
    copies = [
        pltpu.make_async_copy(ids_hbm, ids, sems.at[0]),
        pltpu.make_async_copy(scores_hbm, scores, sems.at[1]),
        pltpu.make_async_copy(
            tokens_hbm.at[pl.ds(pl.multiple_of(head * part, part), part)], mine_ref, sems.at[2]
        ),
    ]
    for copy in copies:
        copy.start()
    copies[0].wait()
    copies[1].wait()
    names, values = ids[...], scores[...]
    top, rows = names.shape
    expert = lax.broadcasted_iota(jnp.int32, (n, rows), 0)
    dense = jnp.zeros((n, rows), jnp.float32)
    for k in range(top):
        dense = dense + jnp.where(expert == names[k : k + 1], values[k : k + 1], 0.0)
    pieces = []
    for _ in range(PIECES):
        piece = dense.astype(jnp.bfloat16).astype(jnp.float32)
        pieces.append(piece)
        dense = dense - piece
    pieces.append(jnp.zeros((LANES - PIECES * n, rows), jnp.float32))
    packed = jnp.concatenate(pieces, axis=0).T
    lanes_ref[...] = jnp.where(head == 0, packed[:part], packed[part:]).astype(jnp.bfloat16)
    lane = lax.broadcasted_iota(jnp.int32, select_ref.shape, 1)
    select_ref[...] = jnp.where(lane % n == expert_ref[0], 1.0, 0.0)
    copies[2].wait()


def spread(head, expert, tokens, expert_ids, gate_scores):
    rows, half_width = tokens.shape
    n = lax.axis_size("wide")
    top = expert_ids.shape[1]
    return pl.pallas_call(
        functools.partial(spread_kernel, n),
        out_shape=[
            jax.ShapeDtypeStruct((rows // 2, half_width), jnp.bfloat16),
            jax.ShapeDtypeStruct((rows // 2, LANES), jnp.bfloat16),
            jax.ShapeDtypeStruct((1, LANES), jnp.float32),
        ],
        in_specs=[pl.BlockSpec(memory_space=pltpu.SMEM)] * 2 + [in_hbm()] * 3,
        out_specs=[in_vmem()] * 3,
        scratch_shapes=[
            pltpu.VMEM((top, rows), jnp.int32),
            pltpu.VMEM((top, rows), jnp.float32),
            pltpu.SemaphoreType.DMA((3,)),
        ],
        compiler_params=pltpu.CompilerParams(vmem_limit_bytes=SMALL_LIMIT),
        cost_estimate=NO_COST,
    )(head, expert, hbm(tokens), hbm(expert_ids.T), hbm(gate_scores.T))


def join_kernel(head_ref, mine_ref, got_ref, lanes_ref, out_ref):
    part, half_width = mine_ref.shape
    first = head_ref[0] == 0
    mine = mine_ref[...]
    out_ref[:, :half_width] = jnp.where(first, mine, got_ref[part:])
    out_ref[:, half_width : 2 * half_width] = jnp.where(first, got_ref[:part], mine)
    out_ref[:, 2 * half_width :] = lanes_ref[...]


def join(head, mine, got, lanes):
    part, half_width = mine.shape
    return pl.pallas_call(
        join_kernel,
        out_shape=jax.ShapeDtypeStruct((part, 2 * half_width + LANES), jnp.bfloat16),
        in_specs=[pl.BlockSpec(memory_space=pltpu.SMEM)] + [in_vmem()] * 3,
        out_specs=in_vmem(),
        compiler_params=pltpu.CompilerParams(vmem_limit_bytes=SMALL_LIMIT),
        cost_estimate=NO_COST,
    )(head, mine, got, lanes)


def gather_kernel(count, _, *refs):
    kept, came = refs[:count], refs[count : 2 * count]
    outs, mark, sems = refs[2 * count : 3 * count], refs[3 * count], refs[3 * count + 1]
    copies = []
    for i in range(count):
        units = kept[i].shape[0]
        cut = units // 2
        for j, (source, target) in enumerate(
            (
                (kept[i].at[:cut], outs[i].at[:cut]),
                (kept[i].at[cut:], outs[i].at[cut:units]),
                (came[i], outs[i].at[units:]),
            )
        ):
            copies.append(pltpu.make_async_copy(source, target, sems.at[i, j]))
    for copy in copies:
        copy.start()
    mark[...] = jnp.zeros(mark.shape, mark.dtype)
    for copy in copies:
        copy.wait()


def gather_weights(mark, kept, came):
    count = len(kept)
    units, width = kept[0].shape
    *whole, mark = pl.pallas_call(
        functools.partial(gather_kernel, count),
        out_shape=[jax.ShapeDtypeStruct((2 * units, width), jnp.bfloat16)] * count
        + [jax.ShapeDtypeStruct(MARK, jnp.float32)],
        in_specs=[pl.BlockSpec(memory_space=pl.ANY)]
        + [in_hbm()] * count
        + [pl.BlockSpec(memory_space=pl.ANY)] * count,
        out_specs=[in_vmem()] * (count + 1),
        scratch_shapes=[pltpu.SemaphoreType.DMA((count, 3))],
        compiler_params=pltpu.CompilerParams(vmem_limit_bytes=SMALL_LIMIT),
        cost_estimate=cost(GATHER_COST),
    )(mark, *[hbm(w) for w in kept], *came)
    return whole, mark


def touch_kernel(*refs):
    refs[-1][...] = jnp.zeros(refs[-1].shape, refs[-1].dtype)


def touch(*values):
    return pl.pallas_call(
        touch_kernel,
        out_shape=jax.ShapeDtypeStruct(MARK, jnp.float32),
        in_specs=[pl.BlockSpec(memory_space=pl.ANY)] * len(values),
        out_specs=in_vmem(),
        compiler_params=pltpu.CompilerParams(vmem_limit_bytes=SMALL_LIMIT),
        cost_estimate=cost(TOUCH_COST),
    )(*values)


def expert_kernel(count, _, select_ref, *refs):
    blocks = refs[:count]
    wg, wu, wd = refs[count : count + 3]
    outs = refs[count + 3 : -1]
    mark = refs[-1]
    width = wg.shape[1]
    whole = [b[...] for b in blocks]
    rows = whole[0] if len(whole) == 1 else jnp.concatenate(whole, axis=0)
    x = rows[:, :width]
    scale = jnp.sum(rows[:, width:].astype(jnp.float32) * select_ref[...], axis=1, keepdims=True)
    contract = (((1,), (1,)), ((), ()))
    gate = lax.dot_general(x, wg[...], contract, preferred_element_type=jnp.float32)
    up = lax.dot_general(x, wu[...], contract, preferred_element_type=jnp.float32)
    hidden = (gate / (1.0 + jnp.exp(-gate)) * up).astype(jnp.bfloat16)
    total = jnp.dot(hidden, wd[...], preferred_element_type=jnp.float32)
    scaled = (total * scale).astype(jnp.bfloat16)
    start = 0
    for out in outs:
        out[...] = scaled[start : start + out.shape[0]]
        start += out.shape[0]
    mark[...] = jnp.zeros(mark.shape, mark.dtype)


def run_expert(mark, groups, select, weights):
    blocks = [b for group in groups for b in group]
    counts = [sum(b.shape[0] for b in group) for group in groups]
    units, width = weights[0].shape
    *outs, mark = pl.pallas_call(
        functools.partial(expert_kernel, len(blocks)),
        out_shape=[jax.ShapeDtypeStruct((c, width), jnp.bfloat16) for c in counts]
        + [jax.ShapeDtypeStruct(MARK, jnp.float32)],
        in_specs=[pl.BlockSpec(memory_space=pl.ANY)]
        + [in_vmem()] * (1 + len(blocks) + len(weights)),
        out_specs=[in_vmem()] * (len(groups) + 1),
        compiler_params=pltpu.CompilerParams(vmem_limit_bytes=VMEM_LIMIT),
        cost_estimate=cost(EXPERT_COST),
    )(mark, select, *blocks, *weights)
    return outs, mark


def add_kernel(_, a_ref, b_ref, out_ref, mark):
    out_ref[...] = (a_ref[...].astype(jnp.float32) + b_ref[...].astype(jnp.float32)).astype(
        jnp.bfloat16
    )
    mark[...] = jnp.zeros(mark.shape, mark.dtype)


def add_rows(mark, a, b):
    return pl.pallas_call(
        add_kernel,
        out_shape=[
            jax.ShapeDtypeStruct(a.shape, jnp.bfloat16),
            jax.ShapeDtypeStruct(MARK, jnp.float32),
        ],
        in_specs=[pl.BlockSpec(memory_space=pl.ANY)] + [in_vmem()] * 2,
        out_specs=[in_vmem()] * 2,
        compiler_params=pltpu.CompilerParams(vmem_limit_bytes=SMALL_LIMIT),
        cost_estimate=cost(ADD_COST),
    )(mark, a, b)


def grow_kernel(count, _, *refs):
    terms, total_ref, mark = refs[:count], refs[count], refs[count + 1]
    total_ref[...] = sum(t[...].astype(jnp.float32) for t in terms)
    mark[...] = jnp.zeros(mark.shape, mark.dtype)


def grow(mark, terms):
    return pl.pallas_call(
        functools.partial(grow_kernel, len(terms)),
        out_shape=[
            jax.ShapeDtypeStruct(terms[0].shape, jnp.float32),
            jax.ShapeDtypeStruct(MARK, jnp.float32),
        ],
        in_specs=[pl.BlockSpec(memory_space=pl.ANY)] + [in_vmem()] * len(terms),
        out_specs=[in_vmem()] * 2,
        compiler_params=pltpu.CompilerParams(vmem_limit_bytes=SMALL_LIMIT),
        cost_estimate=cost(ADD_COST),
    )(mark, *terms)


def collect_kernel(count, head_ref, *refs):
    terms, keep_ref, send_ref = refs[:count], refs[count], refs[count + 1]
    half = keep_ref.shape[1]
    first = head_ref[0] == 0
    total = sum(t[...].astype(jnp.float32) for t in terms).astype(jnp.bfloat16)
    left, right = total[:, :half], total[:, half:]
    keep_ref[...] = jnp.where(first, left, right)
    send_ref[...] = jnp.where(first, right, left)


def collect(head, terms):
    part, width = terms[0].shape
    return pl.pallas_call(
        functools.partial(collect_kernel, len(terms)),
        out_shape=[jax.ShapeDtypeStruct((part, width // 2), jnp.bfloat16)] * 2,
        in_specs=[pl.BlockSpec(memory_space=pltpu.SMEM)] + [in_vmem()] * len(terms),
        out_specs=[in_vmem()] * 2,
        compiler_params=pltpu.CompilerParams(vmem_limit_bytes=SMALL_LIMIT),
        cost_estimate=NO_COST,
    )(head, *terms)


def place_kernel(head_ref, keep_ref, rest_ref, out_ref):
    part = keep_ref.shape[0]
    first = head_ref[0] == 0
    keep, rest = keep_ref[...], rest_ref[...]
    out_ref[:part] = jnp.where(first, keep, rest)
    out_ref[part:] = jnp.where(first, rest, keep)


def place(head, keep, rest):
    part, half_width = keep.shape
    return pl.pallas_call(
        place_kernel,
        out_shape=jax.ShapeDtypeStruct((2 * part, half_width), jnp.bfloat16),
        in_specs=[pl.BlockSpec(memory_space=pltpu.SMEM)] + [in_vmem()] * 2,
        out_specs=in_vmem(),
        compiler_params=pltpu.CompilerParams(vmem_limit_bytes=SMALL_LIMIT),
        cost_estimate=NO_COST,
    )(head, keep, rest)


def after(mark, *values):
    return lax.optimization_barrier((mark, *values))


def dense_local(tokens, expert_ids, gate_scores, gate_proj, up_proj, down_proj):
    n = lax.axis_size("wide")
    head = lax.axis_index("head").reshape(1)
    expert = lax.axis_index("wide").reshape(1)
    tok_rows, half_width = tokens.shape
    part = tok_rows // 2
    swap = ((0, 1), (1, 0))

    def pair(v):
        return lax.ppermute(v, "wide", [(w, w ^ 1) for w in range(n)])

    def column(v, k):
        return lax.ppermute(v, "wide", [(w, w ^ (2 * k)) for w in range(n)])

    def add(*terms):
        return sum(t.astype(jnp.float32) for t in terms).astype(jnp.bfloat16)

    got = lax.ppermute(tokens, "head", swap)
    mine, lanes, select = spread(head, expert, tokens, expert_ids, gate_scores)
    kept = (gate_proj[0], up_proj[0], down_proj[0])
    lanes, got = after(lanes, got)
    own = join(head, mine, got, lanes)

    last = 2
    mid = list(range(3, n // 2))
    got, *held = after(got, *kept)
    came = [lax.ppermute(w, "head", swap) for w in held]
    block = {0: own}
    block.update({k: column(own, k) for k in mid + [1]})
    over = {1: pair(block[1])}
    block[1], own_again = after(block[1], own)
    block[last] = column(own_again, last)
    mark = touch(block[1], *came[:2])
    over[0] = pair(own)
    for k in mid:
        mark, block[k] = after(mark, block[k])
        over[k] = pair(block[k])
    weights, mark = gather_weights(mark, kept, came)
    mark, block[last] = after(mark, block[last])
    over[last] = pair(block[last])

    here, there = {}, {}
    keys = [0] + [1] + mid
    groups = [[v[k]] for v in (block, over) for k in keys]
    done, mark = run_expert(mark, groups, select, weights)
    here.update(zip(keys, done))
    for j, k in enumerate(keys):
        there[k] = pair(done[len(keys) + j])
    keys = [last]
    groups = [[v[k]] for v in (block, over) for k in keys]
    done, mark = run_expert(mark, groups, select, weights)
    here.update(zip(keys, done))
    for j, k in enumerate(keys):
        there[k] = pair(done[len(keys) + j])
    returned = {}
    for k in mid + [1, last]:
        if k in mid + [1]:
            total, mark = add_rows(mark, here[k], there[k])
        else:
            total = add(here[k], there[k])
        returned[k] = column(total, k)
    terms = [here[0], there[0]]
    for k in mid + [1]:
        total, mark = grow(mark, terms + [returned[k]])
        terms = [total]
    terms.append(returned[last])
    keep, send = collect(head, terms)
    rest = lax.ppermute(send, "head", swap)
    return place(head, keep, rest)


def local(tokens, expert_ids, gate_scores, gate_proj, up_proj, down_proj):
    n = lax.axis_size("wide")
    named = expert_ids.shape[1]
    dense = named == n and n >= 8 and n & (n - 1) == 0 and PIECES * n <= LANES
    if dense and lax.axis_size("head") == 2 and tokens.shape[0] % 32 == 0:
        return dense_local(tokens, expert_ids, gate_scores, gate_proj, up_proj, down_proj)
    return sparse_local(tokens, expert_ids, gate_scores, gate_proj, up_proj, down_proj)


def solution(mesh):
    return jax.shard_map(
        local,
        mesh=mesh,
        in_specs=(
            P(("groups", "wide"), "head"),
            P(("groups", "wide"), None),
            P(("groups", "wide"), None),
            P("wide", "head", None),
            P("wide", "head", None),
            P("wide", "head", None),
        ),
        out_specs=P(("groups", "wide"), "head"),
        check_vma=False,
    )
```

```python
import functools

import jax
import jax.numpy as jnp
from jax import lax
from jax.experimental import pallas as pl
from jax.experimental.pallas import tpu as pltpu
from jax.sharding import PartitionSpec as P

LANES = 128
PIECES = 3
VMEM_LIMIT = 16 * 2**20
SMALL_LIMIT = 2 * 2**20
MARK = (8, 128)


def cost(size):
    return pl.CostEstimate(flops=0, bytes_accessed=size, transcendentals=0)


NO_COST = cost(1)
GATHER_COST = 1
TOUCH_COST = 1000000
EXPERT_COST = 1
ADD_COST = 1000000


def sparse_local(tokens, expert_ids, gate_scores, gate_proj, up_proj, down_proj):
    experts = lax.axis_size("wide")
    tok_rows, top_count = expert_ids.shape
    ceiling = (tok_rows * top_count + experts - 1) // experts
    capacity = min(tok_rows, max(2, tok_rows // 8, 2 * ceiling))
    flat_ids = expert_ids.reshape(-1)
    expert_numbers = jnp.arange(experts, dtype=jnp.int32)
    onehot = (flat_ids[:, None] == expert_numbers[None, :]).astype(jnp.int32)
    earlier = jnp.cumsum(onehot, axis=0) - onehot
    slot_index = jnp.sum(earlier * onehot, axis=1)
    position = flat_ids * capacity + slot_index
    targets = jnp.arange(experts * capacity, dtype=jnp.int32)
    placing = jnp.any(
        position.reshape(tok_rows, top_count)[:, :, None] == targets[None, None, :], axis=1
    ).astype(jnp.bfloat16)
    w_gate = gate_proj[0]
    w_up = up_proj[0]
    w_down = down_proj[0]
    placed = lax.dot_general(
        placing, tokens, (((0,), (0,)), ((), ())), preferred_element_type=jnp.float32
    )
    outgoing = placed.astype(jnp.bfloat16).reshape(experts, capacity, tokens.shape[1])
    full_rows = lax.all_gather(
        lax.all_to_all(outgoing, "wide", split_axis=0, concat_axis=0, tiled=True),
        "head",
        axis=2,
        tiled=True,
    )
    src_count, item_count, feature_width = full_rows.shape
    stacked = full_rows.reshape(src_count * item_count, feature_width)
    gate_part = lax.dot_general(
        stacked, w_gate, (((1,), (1,)), ((), ())), preferred_element_type=jnp.float32
    )
    up_part = lax.dot_general(
        stacked, w_up, (((1,), (1,)), ((), ())), preferred_element_type=jnp.float32
    )
    hidden = (jax.nn.silu(gate_part) * up_part).astype(jnp.bfloat16)
    partial_value = jnp.dot(hidden, w_down, preferred_element_type=jnp.float32)
    partial_value = partial_value.reshape(src_count, item_count, feature_width)
    back = lax.psum_scatter(
        partial_value.astype(jnp.bfloat16), "head", scatter_dimension=2, tiled=True
    ).astype(jnp.float32)
    returned = lax.all_to_all(
        back.astype(jnp.bfloat16), "wide", split_axis=0, concat_axis=0, tiled=True
    ).astype(back.dtype)
    picked = returned.reshape(experts * capacity, returned.shape[2])[position]
    picked = picked.reshape(tok_rows, top_count, returned.shape[2])
    mixed = jnp.sum(gate_scores[:, :, None] * picked, axis=1)
    return mixed.astype(jnp.bfloat16)


def in_vmem():
    return pl.BlockSpec(memory_space=pltpu.VMEM)


def in_hbm():
    return pl.BlockSpec(memory_space=pltpu.HBM)


def hbm(v):
    return pltpu.with_memory_space_constraint(v, pltpu.HBM)


def spread_kernel(
    n, head_ref, expert_ref, tokens_hbm, ids_hbm, scores_hbm, mine_ref, lanes_ref, select_ref, ids, scores, sems
):
    part = mine_ref.shape[0]
    head = head_ref[0]
    copies = [
        pltpu.make_async_copy(ids_hbm, ids, sems.at[0]),
        pltpu.make_async_copy(scores_hbm, scores, sems.at[1]),
        pltpu.make_async_copy(
            tokens_hbm.at[pl.ds(pl.multiple_of(head * part, part), part)], mine_ref, sems.at[2]
        ),
    ]
    for copy in copies:
        copy.start()
    copies[0].wait()
    copies[1].wait()
    names, values = ids[...], scores[...]
    top, rows = names.shape
    expert = lax.broadcasted_iota(jnp.int32, (n, rows), 0)
    dense = jnp.zeros((n, rows), jnp.float32)
    for k in range(top):
        dense = dense + jnp.where(expert == names[k : k + 1], values[k : k + 1], 0.0)
    pieces = []
    for _ in range(PIECES):
        piece = dense.astype(jnp.bfloat16).astype(jnp.float32)
        pieces.append(piece)
        dense = dense - piece
    pieces.append(jnp.zeros((LANES - PIECES * n, rows), jnp.float32))
    packed = jnp.concatenate(pieces, axis=0).T
    lanes_ref[...] = jnp.where(head == 0, packed[:part], packed[part:]).astype(jnp.bfloat16)
    lane = lax.broadcasted_iota(jnp.int32, select_ref.shape, 1)
    select_ref[...] = jnp.where(lane % n == expert_ref[0], 1.0, 0.0)
    copies[2].wait()


def spread(head, expert, tokens, expert_ids, gate_scores):
    rows, half_width = tokens.shape
    n = lax.axis_size("wide")
    top = expert_ids.shape[1]
    return pl.pallas_call(
        functools.partial(spread_kernel, n),
        out_shape=[
            jax.ShapeDtypeStruct((rows // 2, half_width), jnp.bfloat16),
            jax.ShapeDtypeStruct((rows // 2, LANES), jnp.bfloat16),
            jax.ShapeDtypeStruct((1, LANES), jnp.float32),
        ],
        in_specs=[pl.BlockSpec(memory_space=pltpu.SMEM)] * 2 + [in_hbm()] * 3,
        out_specs=[in_vmem()] * 3,
        scratch_shapes=[
            pltpu.VMEM((top, rows), jnp.int32),
            pltpu.VMEM((top, rows), jnp.float32),
            pltpu.SemaphoreType.DMA((3,)),
        ],
        compiler_params=pltpu.CompilerParams(vmem_limit_bytes=SMALL_LIMIT),
        cost_estimate=NO_COST,
    )(head, expert, hbm(tokens), hbm(expert_ids.T), hbm(gate_scores.T))


def join_kernel(head_ref, mine_ref, got_ref, lanes_ref, out_ref):
    part, half_width = mine_ref.shape
    first = head_ref[0] == 0
    mine = mine_ref[...]
    out_ref[:, :half_width] = jnp.where(first, mine, got_ref[part:])
    out_ref[:, half_width : 2 * half_width] = jnp.where(first, got_ref[:part], mine)
    out_ref[:, 2 * half_width :] = lanes_ref[...]


def join(head, mine, got, lanes):
    part, half_width = mine.shape
    return pl.pallas_call(
        join_kernel,
        out_shape=jax.ShapeDtypeStruct((part, 2 * half_width + LANES), jnp.bfloat16),
        in_specs=[pl.BlockSpec(memory_space=pltpu.SMEM)] + [in_vmem()] * 3,
        out_specs=in_vmem(),
        compiler_params=pltpu.CompilerParams(vmem_limit_bytes=SMALL_LIMIT),
        cost_estimate=NO_COST,
    )(head, mine, got, lanes)


def gather_kernel(count, _, *refs):
    kept, came = refs[:count], refs[count : 2 * count]
    outs, mark, sems = refs[2 * count : 3 * count], refs[3 * count], refs[3 * count + 1]
    copies = []
    for i in range(count):
        units = kept[i].shape[0]
        cut = units // 2
        for j, (source, target) in enumerate(
            (
                (kept[i].at[:cut], outs[i].at[:cut]),
                (kept[i].at[cut:], outs[i].at[cut:units]),
                (came[i], outs[i].at[units:]),
            )
        ):
            copies.append(pltpu.make_async_copy(source, target, sems.at[i, j]))
    for copy in copies:
        copy.start()
    mark[...] = jnp.zeros(mark.shape, mark.dtype)
    for copy in copies:
        copy.wait()


def gather_weights(mark, kept, came):
    count = len(kept)
    units, width = kept[0].shape
    *whole, mark = pl.pallas_call(
        functools.partial(gather_kernel, count),
        out_shape=[jax.ShapeDtypeStruct((2 * units, width), jnp.bfloat16)] * count
        + [jax.ShapeDtypeStruct(MARK, jnp.float32)],
        in_specs=[pl.BlockSpec(memory_space=pl.ANY)]
        + [in_hbm()] * count
        + [pl.BlockSpec(memory_space=pl.ANY)] * count,
        out_specs=[in_vmem()] * (count + 1),
        scratch_shapes=[pltpu.SemaphoreType.DMA((count, 3))],
        compiler_params=pltpu.CompilerParams(vmem_limit_bytes=SMALL_LIMIT),
        cost_estimate=cost(GATHER_COST),
    )(mark, *[hbm(w) for w in kept], *came)
    return whole, mark


def touch_kernel(*refs):
    refs[-1][...] = jnp.zeros(refs[-1].shape, refs[-1].dtype)


def touch(*values):
    return pl.pallas_call(
        touch_kernel,
        out_shape=jax.ShapeDtypeStruct(MARK, jnp.float32),
        in_specs=[pl.BlockSpec(memory_space=pl.ANY)] * len(values),
        out_specs=in_vmem(),
        compiler_params=pltpu.CompilerParams(vmem_limit_bytes=SMALL_LIMIT),
        cost_estimate=cost(TOUCH_COST),
    )(*values)


def expert_kernel(count, _, select_ref, *refs):
    blocks = refs[:count]
    wg, wu, wd = refs[count : count + 3]
    outs = refs[count + 3 : -1]
    mark = refs[-1]
    width = wg.shape[1]
    whole = [b[...] for b in blocks]
    rows = whole[0] if len(whole) == 1 else jnp.concatenate(whole, axis=0)
    x = rows[:, :width]
    scale = jnp.sum(rows[:, width:].astype(jnp.float32) * select_ref[...], axis=1, keepdims=True)
    contract = (((1,), (1,)), ((), ()))
    gate = lax.dot_general(x, wg[...], contract, preferred_element_type=jnp.float32)
    up = lax.dot_general(x, wu[...], contract, preferred_element_type=jnp.float32)
    hidden = (gate / (1.0 + jnp.exp(-gate)) * up).astype(jnp.bfloat16)
    total = jnp.dot(hidden, wd[...], preferred_element_type=jnp.float32)
    scaled = (total * scale).astype(jnp.bfloat16)
    start = 0
    for out in outs:
        out[...] = scaled[start : start + out.shape[0]]
        start += out.shape[0]
    mark[...] = jnp.zeros(mark.shape, mark.dtype)


def run_expert(mark, groups, select, weights):
    blocks = [b for group in groups for b in group]
    counts = [sum(b.shape[0] for b in group) for group in groups]
    units, width = weights[0].shape
    *outs, mark = pl.pallas_call(
        functools.partial(expert_kernel, len(blocks)),
        out_shape=[jax.ShapeDtypeStruct((c, width), jnp.bfloat16) for c in counts]
        + [jax.ShapeDtypeStruct(MARK, jnp.float32)],
        in_specs=[pl.BlockSpec(memory_space=pl.ANY)]
        + [in_vmem()] * (1 + len(blocks) + len(weights)),
        out_specs=[in_vmem()] * (len(groups) + 1),
        compiler_params=pltpu.CompilerParams(vmem_limit_bytes=VMEM_LIMIT),
        cost_estimate=cost(EXPERT_COST),
    )(mark, select, *blocks, *weights)
    return outs, mark


def add_kernel(_, a_ref, b_ref, out_ref, mark):
    out_ref[...] = (a_ref[...].astype(jnp.float32) + b_ref[...].astype(jnp.float32)).astype(
        jnp.bfloat16
    )
    mark[...] = jnp.zeros(mark.shape, mark.dtype)


def add_rows(mark, a, b):
    return pl.pallas_call(
        add_kernel,
        out_shape=[
            jax.ShapeDtypeStruct(a.shape, jnp.bfloat16),
            jax.ShapeDtypeStruct(MARK, jnp.float32),
        ],
        in_specs=[pl.BlockSpec(memory_space=pl.ANY)] + [in_vmem()] * 2,
        out_specs=[in_vmem()] * 2,
        compiler_params=pltpu.CompilerParams(vmem_limit_bytes=SMALL_LIMIT),
        cost_estimate=cost(ADD_COST),
    )(mark, a, b)


def grow_kernel(count, _, *refs):
    terms, total_ref, mark = refs[:count], refs[count], refs[count + 1]
    total_ref[...] = sum(t[...].astype(jnp.float32) for t in terms)
    mark[...] = jnp.zeros(mark.shape, mark.dtype)


def grow(mark, terms):
    return pl.pallas_call(
        functools.partial(grow_kernel, len(terms)),
        out_shape=[
            jax.ShapeDtypeStruct(terms[0].shape, jnp.float32),
            jax.ShapeDtypeStruct(MARK, jnp.float32),
        ],
        in_specs=[pl.BlockSpec(memory_space=pl.ANY)] + [in_vmem()] * len(terms),
        out_specs=[in_vmem()] * 2,
        compiler_params=pltpu.CompilerParams(vmem_limit_bytes=SMALL_LIMIT),
        cost_estimate=cost(ADD_COST),
    )(mark, *terms)


def collect_kernel(count, head_ref, *refs):
    terms, keep_ref, send_ref = refs[:count], refs[count], refs[count + 1]
    half = keep_ref.shape[1]
    first = head_ref[0] == 0
    total = sum(t[...].astype(jnp.float32) for t in terms).astype(jnp.bfloat16)
    left, right = total[:, :half], total[:, half:]
    keep_ref[...] = jnp.where(first, left, right)
    send_ref[...] = jnp.where(first, right, left)


def collect(head, terms):
    part, width = terms[0].shape
    return pl.pallas_call(
        functools.partial(collect_kernel, len(terms)),
        out_shape=[jax.ShapeDtypeStruct((part, width // 2), jnp.bfloat16)] * 2,
        in_specs=[pl.BlockSpec(memory_space=pltpu.SMEM)] + [in_vmem()] * len(terms),
        out_specs=[in_vmem()] * 2,
        compiler_params=pltpu.CompilerParams(vmem_limit_bytes=SMALL_LIMIT),
        cost_estimate=NO_COST,
    )(head, *terms)


def place_kernel(head_ref, keep_ref, rest_ref, out_ref):
    part = keep_ref.shape[0]
    first = head_ref[0] == 0
    keep, rest = keep_ref[...], rest_ref[...]
    out_ref[:part] = jnp.where(first, keep, rest)
    out_ref[part:] = jnp.where(first, rest, keep)


def place(head, keep, rest):
    part, half_width = keep.shape
    return pl.pallas_call(
        place_kernel,
        out_shape=jax.ShapeDtypeStruct((2 * part, half_width), jnp.bfloat16),
        in_specs=[pl.BlockSpec(memory_space=pltpu.SMEM)] + [in_vmem()] * 2,
        out_specs=in_vmem(),
        compiler_params=pltpu.CompilerParams(vmem_limit_bytes=SMALL_LIMIT),
        cost_estimate=NO_COST,
    )(head, keep, rest)


def after(mark, *values):
    return lax.optimization_barrier((mark, *values))


def dense_local(tokens, expert_ids, gate_scores, gate_proj, up_proj, down_proj):
    n = lax.axis_size("wide")
    head = lax.axis_index("head").reshape(1)
    expert = lax.axis_index("wide").reshape(1)
    tok_rows, half_width = tokens.shape
    part = tok_rows // 2
    swap = ((0, 1), (1, 0))

    def pair(v):
        return lax.ppermute(v, "wide", [(w, w ^ 1) for w in range(n)])

    def column(v, k):
        return lax.ppermute(v, "wide", [(w, w ^ (2 * k)) for w in range(n)])

    def add(*terms):
        return sum(t.astype(jnp.float32) for t in terms).astype(jnp.bfloat16)

    got = lax.ppermute(tokens, "head", swap)
    mine, lanes, select = spread(head, expert, tokens, expert_ids, gate_scores)
    kept = (gate_proj[0], up_proj[0], down_proj[0])
    lanes, got = after(lanes, got)
    own = join(head, mine, got, lanes)

    last = 2
    mid = list(range(3, n // 2))
    got, *held = after(got, *kept)
    came = [lax.ppermute(w, "head", swap) for w in held]
    block = {0: own}
    block.update({k: column(own, k) for k in mid + [1]})
    over = {}
    over[1] = pair(block[1])
    block[1], own_again = after(block[1], own)
    block[last] = column(own_again, last)
    mark = touch(block[1], *came[:2])
    over[0] = pair(own)
    for k in mid:
        mark, block[k] = after(mark, block[k])
        over[k] = pair(block[k])
    weights, mark = gather_weights(mark, kept, came)
    mark, block[last] = after(mark, block[last])
    over[last] = pair(block[last])

    here, there = {}, {}
    keys = [0] + [1] + mid
    groups = [[v[k]] for v in (block, over) for k in keys]
    done, mark = run_expert(mark, groups, select, weights)
    here.update(zip(keys, done))
    for j, k in enumerate(keys):
        there[k] = done[len(keys) + j]
        if k >= 2:
            there[k] = pair(there[k])
    keys = [last]
    groups = [[v[k]] for v in (block, over) for k in keys]
    done, mark = run_expert(mark, groups, select, weights)
    here.update(zip(keys, done))
    for j, k in enumerate(keys):
        there[k] = done[len(keys) + j]
        if k >= 2:
            there[k] = pair(there[k])
    returned = {}
    for k in mid:
        total, mark = add_rows(mark, here[k], there[k])
        returned[k] = column(total, k)
        for j in (1, 0):
            mark, there[j] = after(mark, there[j])
            there[j] = pair(there[j])
    total = add(here[last], there[last])
    returned[last] = column(total, last)
    total, mark = grow(mark, [here[0]] + [returned[k] for k in mid])
    first, mark = add_rows(mark, here[1], there[1])
    returned[1] = column(first, 1)
    total, mark = grow(mark, [total, there[0]])
    terms = [total, returned[1], returned[last]]
    keep, send = collect(head, terms)
    rest = lax.ppermute(send, "head", swap)
    return place(head, keep, rest)


def local(tokens, expert_ids, gate_scores, gate_proj, up_proj, down_proj):
    n = lax.axis_size("wide")
    named = expert_ids.shape[1]
    dense = named == n and n >= 8 and n & (n - 1) == 0 and PIECES * n <= LANES
    if dense and lax.axis_size("head") == 2 and tokens.shape[0] % 32 == 0:
        return dense_local(tokens, expert_ids, gate_scores, gate_proj, up_proj, down_proj)
    return sparse_local(tokens, expert_ids, gate_scores, gate_proj, up_proj, down_proj)


def solution(mesh):
    return jax.shard_map(
        local,
        mesh=mesh,
        in_specs=(
            P(("groups", "wide"), "head"),
            P(("groups", "wide"), None),
            P(("groups", "wide"), None),
            P("wide", "head", None),
            P("wide", "head", None),
            P("wide", "head", None),
        ),
        out_specs=P(("groups", "wide"), "head"),
        check_vma=False,
    )
```

```python
import functools

import jax
import jax.numpy as jnp
from jax import lax
from jax.experimental import pallas as pl
from jax.experimental.pallas import tpu as pltpu
from jax.sharding import PartitionSpec as P

LANES = 128
PIECES = 3
VMEM_LIMIT = 16 * 2**20
SMALL_LIMIT = 2 * 2**20
MARK = (8, 128)


def cost(size):
    return pl.CostEstimate(flops=0, bytes_accessed=size, transcendentals=0)


NO_COST = cost(1)
GATHER_COST = 1
TOUCH_COST = 1000000
EXPERT_COST = 1


def sparse_local(tokens, expert_ids, gate_scores, gate_proj, up_proj, down_proj):
    experts = lax.axis_size("wide")
    tok_rows, top_count = expert_ids.shape
    ceiling = (tok_rows * top_count + experts - 1) // experts
    capacity = min(tok_rows, max(2, tok_rows // 8, 2 * ceiling))
    flat_ids = expert_ids.reshape(-1)
    expert_numbers = jnp.arange(experts, dtype=jnp.int32)
    onehot = (flat_ids[:, None] == expert_numbers[None, :]).astype(jnp.int32)
    earlier = jnp.cumsum(onehot, axis=0) - onehot
    slot_index = jnp.sum(earlier * onehot, axis=1)
    position = flat_ids * capacity + slot_index
    targets = jnp.arange(experts * capacity, dtype=jnp.int32)
    placing = jnp.any(
        position.reshape(tok_rows, top_count)[:, :, None] == targets[None, None, :], axis=1
    ).astype(jnp.bfloat16)
    w_gate = gate_proj[0]
    w_up = up_proj[0]
    w_down = down_proj[0]
    placed = lax.dot_general(
        placing, tokens, (((0,), (0,)), ((), ())), preferred_element_type=jnp.float32
    )
    outgoing = placed.astype(jnp.bfloat16).reshape(experts, capacity, tokens.shape[1])
    full_rows = lax.all_gather(
        lax.all_to_all(outgoing, "wide", split_axis=0, concat_axis=0, tiled=True),
        "head",
        axis=2,
        tiled=True,
    )
    src_count, item_count, feature_width = full_rows.shape
    stacked = full_rows.reshape(src_count * item_count, feature_width)
    gate_part = lax.dot_general(
        stacked, w_gate, (((1,), (1,)), ((), ())), preferred_element_type=jnp.float32
    )
    up_part = lax.dot_general(
        stacked, w_up, (((1,), (1,)), ((), ())), preferred_element_type=jnp.float32
    )
    hidden = (jax.nn.silu(gate_part) * up_part).astype(jnp.bfloat16)
    partial_value = jnp.dot(hidden, w_down, preferred_element_type=jnp.float32)
    partial_value = partial_value.reshape(src_count, item_count, feature_width)
    back = lax.psum_scatter(
        partial_value.astype(jnp.bfloat16), "head", scatter_dimension=2, tiled=True
    ).astype(jnp.float32)
    returned = lax.all_to_all(
        back.astype(jnp.bfloat16), "wide", split_axis=0, concat_axis=0, tiled=True
    ).astype(back.dtype)
    picked = returned.reshape(experts * capacity, returned.shape[2])[position]
    picked = picked.reshape(tok_rows, top_count, returned.shape[2])
    mixed = jnp.sum(gate_scores[:, :, None] * picked, axis=1)
    return mixed.astype(jnp.bfloat16)


def in_vmem():
    return pl.BlockSpec(memory_space=pltpu.VMEM)


def in_hbm():
    return pl.BlockSpec(memory_space=pltpu.HBM)


def hbm(v):
    return pltpu.with_memory_space_constraint(v, pltpu.HBM)


def spread_kernel(
    n, head_ref, expert_ref, tokens_hbm, ids_hbm, scores_hbm, mine_ref, lanes_ref, select_ref, ids, scores, sems
):
    part = mine_ref.shape[0]
    head = head_ref[0]
    copies = [
        pltpu.make_async_copy(ids_hbm, ids, sems.at[0]),
        pltpu.make_async_copy(scores_hbm, scores, sems.at[1]),
        pltpu.make_async_copy(
            tokens_hbm.at[pl.ds(pl.multiple_of(head * part, part), part)], mine_ref, sems.at[2]
        ),
    ]
    for copy in copies:
        copy.start()
    copies[0].wait()
    copies[1].wait()
    names, values = ids[...], scores[...]
    top, rows = names.shape
    expert = lax.broadcasted_iota(jnp.int32, (n, rows), 0)
    dense = jnp.zeros((n, rows), jnp.float32)
    for k in range(top):
        dense = dense + jnp.where(expert == names[k : k + 1], values[k : k + 1], 0.0)
    pieces = []
    for _ in range(PIECES):
        piece = dense.astype(jnp.bfloat16).astype(jnp.float32)
        pieces.append(piece)
        dense = dense - piece
    pieces.append(jnp.zeros((LANES - PIECES * n, rows), jnp.float32))
    packed = jnp.concatenate(pieces, axis=0).T
    lanes_ref[...] = jnp.where(head == 0, packed[:part], packed[part:]).astype(jnp.bfloat16)
    lane = lax.broadcasted_iota(jnp.int32, select_ref.shape, 1)
    select_ref[...] = jnp.where(lane % n == expert_ref[0], 1.0, 0.0)
    copies[2].wait()


def spread(head, expert, tokens, expert_ids, gate_scores):
    rows, half_width = tokens.shape
    n = lax.axis_size("wide")
    top = expert_ids.shape[1]
    return pl.pallas_call(
        functools.partial(spread_kernel, n),
        out_shape=[
            jax.ShapeDtypeStruct((rows // 2, half_width), jnp.bfloat16),
            jax.ShapeDtypeStruct((rows // 2, LANES), jnp.bfloat16),
            jax.ShapeDtypeStruct((1, LANES), jnp.float32),
        ],
        in_specs=[pl.BlockSpec(memory_space=pltpu.SMEM)] * 2 + [in_hbm()] * 3,
        out_specs=[in_vmem()] * 3,
        scratch_shapes=[
            pltpu.VMEM((top, rows), jnp.int32),
            pltpu.VMEM((top, rows), jnp.float32),
            pltpu.SemaphoreType.DMA((3,)),
        ],
        compiler_params=pltpu.CompilerParams(vmem_limit_bytes=SMALL_LIMIT),
        cost_estimate=NO_COST,
    )(head, expert, hbm(tokens), hbm(expert_ids.T), hbm(gate_scores.T))


def join_kernel(head_ref, mine_ref, got_ref, lanes_ref, out_ref):
    part, half_width = mine_ref.shape
    first = head_ref[0] == 0
    mine = mine_ref[...]
    out_ref[:, :half_width] = jnp.where(first, mine, got_ref[part:])
    out_ref[:, half_width : 2 * half_width] = jnp.where(first, got_ref[:part], mine)
    out_ref[:, 2 * half_width :] = lanes_ref[...]


def join(head, mine, got, lanes):
    part, half_width = mine.shape
    return pl.pallas_call(
        join_kernel,
        out_shape=jax.ShapeDtypeStruct((part, 2 * half_width + LANES), jnp.bfloat16),
        in_specs=[pl.BlockSpec(memory_space=pltpu.SMEM)] + [in_vmem()] * 3,
        out_specs=in_vmem(),
        compiler_params=pltpu.CompilerParams(vmem_limit_bytes=SMALL_LIMIT),
        cost_estimate=NO_COST,
    )(head, mine, got, lanes)


def gather_kernel(count, _, *refs):
    kept, came = refs[:count], refs[count : 2 * count]
    outs, mark, sems = refs[2 * count : 3 * count], refs[3 * count], refs[3 * count + 1]
    copies = []
    for i in range(count):
        units = kept[i].shape[0]
        cut = units // 2
        for j, (source, target) in enumerate(
            (
                (kept[i].at[:cut], outs[i].at[:cut]),
                (kept[i].at[cut:], outs[i].at[cut:units]),
                (came[i], outs[i].at[units:]),
            )
        ):
            copies.append(pltpu.make_async_copy(source, target, sems.at[i, j]))
    for copy in copies:
        copy.start()
    mark[...] = jnp.zeros(mark.shape, mark.dtype)
    for copy in copies:
        copy.wait()


def gather_weights(mark, kept, came):
    count = len(kept)
    units, width = kept[0].shape
    *whole, mark = pl.pallas_call(
        functools.partial(gather_kernel, count),
        out_shape=[jax.ShapeDtypeStruct((2 * units, width), jnp.bfloat16)] * count
        + [jax.ShapeDtypeStruct(MARK, jnp.float32)],
        in_specs=[pl.BlockSpec(memory_space=pl.ANY)]
        + [in_hbm()] * count
        + [pl.BlockSpec(memory_space=pl.ANY)] * count,
        out_specs=[in_vmem()] * (count + 1),
        scratch_shapes=[pltpu.SemaphoreType.DMA((count, 3))],
        compiler_params=pltpu.CompilerParams(vmem_limit_bytes=SMALL_LIMIT),
        cost_estimate=cost(GATHER_COST),
    )(mark, *[hbm(w) for w in kept], *came)
    return whole, mark


def touch_kernel(*refs):
    refs[-1][...] = jnp.zeros(refs[-1].shape, refs[-1].dtype)


def touch(*values):
    return pl.pallas_call(
        touch_kernel,
        out_shape=jax.ShapeDtypeStruct(MARK, jnp.float32),
        in_specs=[pl.BlockSpec(memory_space=pl.ANY)] * len(values),
        out_specs=in_vmem(),
        compiler_params=pltpu.CompilerParams(vmem_limit_bytes=SMALL_LIMIT),
        cost_estimate=cost(TOUCH_COST),
    )(*values)


def expert_kernel(count, _, select_ref, *refs):
    blocks = refs[:count]
    wg, wu, wd = refs[count : count + 3]
    outs = refs[count + 3 : -1]
    mark = refs[-1]
    width = wg.shape[1]
    whole = [b[...] for b in blocks]
    rows = whole[0] if len(whole) == 1 else jnp.concatenate(whole, axis=0)
    x = rows[:, :width]
    scale = jnp.sum(rows[:, width:].astype(jnp.float32) * select_ref[...], axis=1, keepdims=True)
    contract = (((1,), (1,)), ((), ()))
    gate = lax.dot_general(x, wg[...], contract, preferred_element_type=jnp.float32)
    up = lax.dot_general(x, wu[...], contract, preferred_element_type=jnp.float32)
    hidden = (gate / (1.0 + jnp.exp(-gate)) * up).astype(jnp.bfloat16)
    total = jnp.dot(hidden, wd[...], preferred_element_type=jnp.float32)
    scaled = (total * scale).astype(jnp.bfloat16)
    start = 0
    for out in outs:
        out[...] = scaled[start : start + out.shape[0]]
        start += out.shape[0]
    mark[...] = jnp.zeros(mark.shape, mark.dtype)


def run_expert(mark, groups, select, weights):
    blocks = [b for group in groups for b in group]
    counts = [sum(b.shape[0] for b in group) for group in groups]
    units, width = weights[0].shape
    *outs, mark = pl.pallas_call(
        functools.partial(expert_kernel, len(blocks)),
        out_shape=[jax.ShapeDtypeStruct((c, width), jnp.bfloat16) for c in counts]
        + [jax.ShapeDtypeStruct(MARK, jnp.float32)],
        in_specs=[pl.BlockSpec(memory_space=pl.ANY)]
        + [in_vmem()] * (1 + len(blocks) + len(weights)),
        out_specs=[in_vmem()] * (len(groups) + 1),
        compiler_params=pltpu.CompilerParams(vmem_limit_bytes=VMEM_LIMIT),
        cost_estimate=cost(EXPERT_COST),
    )(mark, select, *blocks, *weights)
    return outs, mark


def collect_kernel(count, head_ref, _, *refs):
    terms, keep_ref, send_ref = refs[:count], refs[count], refs[count + 1]
    half = keep_ref.shape[1]
    first = head_ref[0] == 0
    total = sum(t[...].astype(jnp.float32) for t in terms).astype(jnp.bfloat16)
    left, right = total[:, :half], total[:, half:]
    keep_ref[...] = jnp.where(first, left, right)
    send_ref[...] = jnp.where(first, right, left)


def collect(head, mark, terms):
    part, width = terms[0].shape
    return pl.pallas_call(
        functools.partial(collect_kernel, len(terms)),
        out_shape=[jax.ShapeDtypeStruct((part, width // 2), jnp.bfloat16)] * 2,
        in_specs=[pl.BlockSpec(memory_space=pltpu.SMEM), pl.BlockSpec(memory_space=pl.ANY)]
        + [in_vmem()] * len(terms),
        out_specs=[in_vmem()] * 2,
        compiler_params=pltpu.CompilerParams(vmem_limit_bytes=SMALL_LIMIT),
        cost_estimate=NO_COST,
    )(head, mark, *terms)


def place_kernel(head_ref, keep_ref, rest_ref, out_ref):
    part = keep_ref.shape[0]
    first = head_ref[0] == 0
    keep, rest = keep_ref[...], rest_ref[...]
    out_ref[:part] = jnp.where(first, keep, rest)
    out_ref[part:] = jnp.where(first, rest, keep)


def place(head, keep, rest):
    part, half_width = keep.shape
    return pl.pallas_call(
        place_kernel,
        out_shape=jax.ShapeDtypeStruct((2 * part, half_width), jnp.bfloat16),
        in_specs=[pl.BlockSpec(memory_space=pltpu.SMEM)] + [in_vmem()] * 2,
        out_specs=in_vmem(),
        compiler_params=pltpu.CompilerParams(vmem_limit_bytes=SMALL_LIMIT),
        cost_estimate=NO_COST,
    )(head, keep, rest)


def after(mark, *values):
    return lax.optimization_barrier((mark, *values))


def dense_local(tokens, expert_ids, gate_scores, gate_proj, up_proj, down_proj):
    n = lax.axis_size("wide")
    head = lax.axis_index("head").reshape(1)
    expert = lax.axis_index("wide").reshape(1)
    tok_rows, half_width = tokens.shape
    part = tok_rows // 2
    swap = ((0, 1), (1, 0))

    def pair(v):
        return lax.ppermute(v, "wide", [(w, w ^ 1) for w in range(n)])

    def column(v, k):
        return lax.ppermute(v, "wide", [(w, w ^ (2 * k)) for w in range(n)])

    def add(*terms):
        return sum(t.astype(jnp.float32) for t in terms).astype(jnp.bfloat16)

    got = lax.ppermute(tokens, "head", swap)
    mine, lanes, select = spread(head, expert, tokens, expert_ids, gate_scores)
    kept = (gate_proj[0], up_proj[0], down_proj[0])
    lanes, got = after(lanes, got)
    own = join(head, mine, got, lanes)

    last = 2
    mid = list(range(3, n // 2))
    got, *held = after(got, *kept)
    came = [lax.ppermute(w, "head", swap) for w in held]
    block = {0: own}
    block.update({k: column(own, k) for k in mid + [1]})
    over = {}
    over[1] = pair(block[1])
    block[1], own_again = after(block[1], own)
    block[last] = column(own_again, last)
    mark = touch(block[1], *came[:2])
    over[0] = pair(own)
    for k in mid:
        mark, block[k] = after(mark, block[k])
        over[k] = pair(block[k])
    weights, mark = gather_weights(mark, kept, came)
    mark, block[last] = after(mark, block[last])
    over[last] = pair(block[last])

    here, there = {}, {}
    keys = [0] + [1] + mid
    groups = [[v[k]] for v in (block, over) for k in keys]
    done, mark = run_expert(mark, groups, select, weights)
    here.update(zip(keys, done))
    for j, k in enumerate(keys):
        there[k] = done[len(keys) + j]
        if k >= 2:
            there[k] = pair(there[k])
    keys = [last]
    groups = [[v[k]] for v in (block, over) for k in keys]
    done, mark = run_expert(mark, groups, select, weights)
    here.update(zip(keys, done))
    for j, k in enumerate(keys):
        there[k] = done[len(keys) + j]
        if k >= 2:
            there[k] = pair(there[k])
    returned = {}
    for k in mid:
        returned[k] = column(add(here[k], there[k]), k)
        mark = touch(mark, there[k])
    for k in (1, 0):
        mark, there[k] = after(mark, there[k])
        there[k] = pair(there[k])
    returned[last] = column(add(here[last], there[last]), last)
    mark = touch(mark, *[returned[k] for k in mid])
    mark, there[1] = after(mark, there[1])
    returned[1] = column(add(here[1], there[1]), 1)
    terms = [here[0], there[0], *returned.values()]
    keep, send = collect(head, mark, terms)
    rest = lax.ppermute(send, "head", swap)
    return place(head, keep, rest)


def local(tokens, expert_ids, gate_scores, gate_proj, up_proj, down_proj):
    n = lax.axis_size("wide")
    named = expert_ids.shape[1]
    dense = named == n and n >= 8 and n & (n - 1) == 0 and PIECES * n <= LANES
    if dense and lax.axis_size("head") == 2 and tokens.shape[0] % 32 == 0:
        return dense_local(tokens, expert_ids, gate_scores, gate_proj, up_proj, down_proj)
    return sparse_local(tokens, expert_ids, gate_scores, gate_proj, up_proj, down_proj)


def solution(mesh):
    return jax.shard_map(
        local,
        mesh=mesh,
        in_specs=(
            P(("groups", "wide"), "head"),
            P(("groups", "wide"), None),
            P(("groups", "wide"), None),
            P("wide", "head", None),
            P("wide", "head", None),
            P("wide", "head", None),
        ),
        out_specs=P(("groups", "wide"), "head"),
        check_vma=False,
    )
```

```python
import functools

import jax
import jax.numpy as jnp
from jax import lax
from jax.experimental import pallas as pl
from jax.experimental.pallas import tpu as pltpu
from jax.sharding import PartitionSpec as P

LANES = 128
PIECES = 3
VMEM_LIMIT = 16 * 2**20
SMALL_LIMIT = 2 * 2**20
MARK = (8, 128)


def cost(size):
    return pl.CostEstimate(flops=0, bytes_accessed=size, transcendentals=0)


NO_COST = cost(1)
GATHER_COST = 1
TOUCH_COST = 1000000
EXPERT_COST = 1


def sparse_local(tokens, expert_ids, gate_scores, gate_proj, up_proj, down_proj):
    experts = lax.axis_size("wide")
    tok_rows, top_count = expert_ids.shape
    ceiling = (tok_rows * top_count + experts - 1) // experts
    capacity = min(tok_rows, max(2, tok_rows // 8, 2 * ceiling))
    flat_ids = expert_ids.reshape(-1)
    expert_numbers = jnp.arange(experts, dtype=jnp.int32)
    onehot = (flat_ids[:, None] == expert_numbers[None, :]).astype(jnp.int32)
    earlier = jnp.cumsum(onehot, axis=0) - onehot
    slot_index = jnp.sum(earlier * onehot, axis=1)
    position = flat_ids * capacity + slot_index
    targets = jnp.arange(experts * capacity, dtype=jnp.int32)
    placing = jnp.any(
        position.reshape(tok_rows, top_count)[:, :, None] == targets[None, None, :], axis=1
    ).astype(jnp.bfloat16)
    w_gate = gate_proj[0]
    w_up = up_proj[0]
    w_down = down_proj[0]
    placed = lax.dot_general(
        placing, tokens, (((0,), (0,)), ((), ())), preferred_element_type=jnp.float32
    )
    outgoing = placed.astype(jnp.bfloat16).reshape(experts, capacity, tokens.shape[1])
    full_rows = lax.all_gather(
        lax.all_to_all(outgoing, "wide", split_axis=0, concat_axis=0, tiled=True),
        "head",
        axis=2,
        tiled=True,
    )
    src_count, item_count, feature_width = full_rows.shape
    stacked = full_rows.reshape(src_count * item_count, feature_width)
    gate_part = lax.dot_general(
        stacked, w_gate, (((1,), (1,)), ((), ())), preferred_element_type=jnp.float32
    )
    up_part = lax.dot_general(
        stacked, w_up, (((1,), (1,)), ((), ())), preferred_element_type=jnp.float32
    )
    hidden = (jax.nn.silu(gate_part) * up_part).astype(jnp.bfloat16)
    partial_value = jnp.dot(hidden, w_down, preferred_element_type=jnp.float32)
    partial_value = partial_value.reshape(src_count, item_count, feature_width)
    back = lax.psum_scatter(
        partial_value.astype(jnp.bfloat16), "head", scatter_dimension=2, tiled=True
    ).astype(jnp.float32)
    returned = lax.all_to_all(
        back.astype(jnp.bfloat16), "wide", split_axis=0, concat_axis=0, tiled=True
    ).astype(back.dtype)
    picked = returned.reshape(experts * capacity, returned.shape[2])[position]
    picked = picked.reshape(tok_rows, top_count, returned.shape[2])
    mixed = jnp.sum(gate_scores[:, :, None] * picked, axis=1)
    return mixed.astype(jnp.bfloat16)


def in_vmem():
    return pl.BlockSpec(memory_space=pltpu.VMEM)


def in_hbm():
    return pl.BlockSpec(memory_space=pltpu.HBM)


def hbm(v):
    return pltpu.with_memory_space_constraint(v, pltpu.HBM)


def spread_kernel(
    n, head_ref, expert_ref, tokens_hbm, ids_hbm, scores_hbm, mine_ref, lanes_ref, select_ref, ids, scores, sems
):
    part = mine_ref.shape[0]
    head = head_ref[0]
    copies = [
        pltpu.make_async_copy(ids_hbm, ids, sems.at[0]),
        pltpu.make_async_copy(scores_hbm, scores, sems.at[1]),
        pltpu.make_async_copy(
            tokens_hbm.at[pl.ds(pl.multiple_of(head * part, part), part)], mine_ref, sems.at[2]
        ),
    ]
    for copy in copies:
        copy.start()
    copies[0].wait()
    copies[1].wait()
    names, values = ids[...], scores[...]
    top, rows = names.shape
    expert = lax.broadcasted_iota(jnp.int32, (n, rows), 0)
    dense = jnp.zeros((n, rows), jnp.float32)
    for k in range(top):
        dense = dense + jnp.where(expert == names[k : k + 1], values[k : k + 1], 0.0)
    pieces = []
    for _ in range(PIECES):
        piece = dense.astype(jnp.bfloat16).astype(jnp.float32)
        pieces.append(piece)
        dense = dense - piece
    pieces.append(jnp.zeros((LANES - PIECES * n, rows), jnp.float32))
    packed = jnp.concatenate(pieces, axis=0).T
    lanes_ref[...] = jnp.where(head == 0, packed[:part], packed[part:]).astype(jnp.bfloat16)
    lane = lax.broadcasted_iota(jnp.int32, select_ref.shape, 1)
    select_ref[...] = jnp.where(lane % n == expert_ref[0], 1.0, 0.0)
    copies[2].wait()


def spread(head, expert, tokens, expert_ids, gate_scores):
    rows, half_width = tokens.shape
    n = lax.axis_size("wide")
    top = expert_ids.shape[1]
    return pl.pallas_call(
        functools.partial(spread_kernel, n),
        out_shape=[
            jax.ShapeDtypeStruct((rows // 2, half_width), jnp.bfloat16),
            jax.ShapeDtypeStruct((rows // 2, LANES), jnp.bfloat16),
            jax.ShapeDtypeStruct((1, LANES), jnp.float32),
        ],
        in_specs=[pl.BlockSpec(memory_space=pltpu.SMEM)] * 2 + [in_hbm()] * 3,
        out_specs=[in_vmem()] * 3,
        scratch_shapes=[
            pltpu.VMEM((top, rows), jnp.int32),
            pltpu.VMEM((top, rows), jnp.float32),
            pltpu.SemaphoreType.DMA((3,)),
        ],
        compiler_params=pltpu.CompilerParams(vmem_limit_bytes=SMALL_LIMIT),
        cost_estimate=NO_COST,
    )(head, expert, hbm(tokens), hbm(expert_ids.T), hbm(gate_scores.T))


def join_kernel(head_ref, mine_ref, got_ref, lanes_ref, out_ref):
    part, half_width = mine_ref.shape
    first = head_ref[0] == 0
    mine = mine_ref[...]
    out_ref[:, :half_width] = jnp.where(first, mine, got_ref[part:])
    out_ref[:, half_width : 2 * half_width] = jnp.where(first, got_ref[:part], mine)
    out_ref[:, 2 * half_width :] = lanes_ref[...]


def join(head, mine, got, lanes):
    part, half_width = mine.shape
    return pl.pallas_call(
        join_kernel,
        out_shape=jax.ShapeDtypeStruct((part, 2 * half_width + LANES), jnp.bfloat16),
        in_specs=[pl.BlockSpec(memory_space=pltpu.SMEM)] + [in_vmem()] * 3,
        out_specs=in_vmem(),
        compiler_params=pltpu.CompilerParams(vmem_limit_bytes=SMALL_LIMIT),
        cost_estimate=NO_COST,
    )(head, mine, got, lanes)


def gather_kernel(count, _, *refs):
    kept, came = refs[:count], refs[count : 2 * count]
    outs, mark, sems = refs[2 * count : 3 * count], refs[3 * count], refs[3 * count + 1]
    copies = []
    for i in range(count):
        units = kept[i].shape[0]
        cut = units // 2
        for j, (source, target) in enumerate(
            (
                (kept[i].at[:cut], outs[i].at[:cut]),
                (kept[i].at[cut:], outs[i].at[cut:units]),
                (came[i], outs[i].at[units:]),
            )
        ):
            copies.append(pltpu.make_async_copy(source, target, sems.at[i, j]))
    for copy in copies:
        copy.start()
    mark[...] = jnp.zeros(mark.shape, mark.dtype)
    for copy in copies:
        copy.wait()


def gather_weights(mark, kept, came):
    count = len(kept)
    units, width = kept[0].shape
    *whole, mark = pl.pallas_call(
        functools.partial(gather_kernel, count),
        out_shape=[jax.ShapeDtypeStruct((2 * units, width), jnp.bfloat16)] * count
        + [jax.ShapeDtypeStruct(MARK, jnp.float32)],
        in_specs=[pl.BlockSpec(memory_space=pl.ANY)]
        + [in_hbm()] * count
        + [pl.BlockSpec(memory_space=pl.ANY)] * count,
        out_specs=[in_vmem()] * (count + 1),
        scratch_shapes=[pltpu.SemaphoreType.DMA((count, 3))],
        compiler_params=pltpu.CompilerParams(vmem_limit_bytes=SMALL_LIMIT),
        cost_estimate=cost(GATHER_COST),
    )(mark, *[hbm(w) for w in kept], *came)
    return whole, mark


def touch_kernel(*refs):
    refs[-1][...] = jnp.zeros(refs[-1].shape, refs[-1].dtype)


def touch(*values):
    return pl.pallas_call(
        touch_kernel,
        out_shape=jax.ShapeDtypeStruct(MARK, jnp.float32),
        in_specs=[pl.BlockSpec(memory_space=pl.ANY)] * len(values),
        out_specs=in_vmem(),
        compiler_params=pltpu.CompilerParams(vmem_limit_bytes=SMALL_LIMIT),
        cost_estimate=cost(TOUCH_COST),
    )(*values)


def expert_kernel(count, _, select_ref, *refs):
    blocks = refs[:count]
    wg, wu, wd = refs[count : count + 3]
    outs = refs[count + 3 : -1]
    mark = refs[-1]
    width = wg.shape[1]
    whole = [b[...] for b in blocks]
    rows = whole[0] if len(whole) == 1 else jnp.concatenate(whole, axis=0)
    x = rows[:, :width]
    scale = jnp.sum(rows[:, width:].astype(jnp.float32) * select_ref[...], axis=1, keepdims=True)
    contract = (((1,), (1,)), ((), ()))
    gate = lax.dot_general(x, wg[...], contract, preferred_element_type=jnp.float32)
    up = lax.dot_general(x, wu[...], contract, preferred_element_type=jnp.float32)
    hidden = (gate / (1.0 + jnp.exp(-gate)) * up).astype(jnp.bfloat16)
    total = jnp.dot(hidden, wd[...], preferred_element_type=jnp.float32)
    scaled = (total * scale).astype(jnp.bfloat16)
    start = 0
    for out in outs:
        out[...] = scaled[start : start + out.shape[0]]
        start += out.shape[0]
    mark[...] = jnp.zeros(mark.shape, mark.dtype)


def run_expert(mark, groups, select, weights):
    blocks = [b for group in groups for b in group]
    counts = [sum(b.shape[0] for b in group) for group in groups]
    units, width = weights[0].shape
    *outs, mark = pl.pallas_call(
        functools.partial(expert_kernel, len(blocks)),
        out_shape=[jax.ShapeDtypeStruct((c, width), jnp.bfloat16) for c in counts]
        + [jax.ShapeDtypeStruct(MARK, jnp.float32)],
        in_specs=[pl.BlockSpec(memory_space=pl.ANY)]
        + [in_vmem()] * (1 + len(blocks) + len(weights)),
        out_specs=[in_vmem()] * (len(groups) + 1),
        compiler_params=pltpu.CompilerParams(vmem_limit_bytes=VMEM_LIMIT),
        cost_estimate=cost(EXPERT_COST),
    )(mark, select, *blocks, *weights)
    return outs, mark


def collect_kernel(count, head_ref, _, *refs):
    terms, keep_ref, send_ref = refs[:count], refs[count], refs[count + 1]
    half = keep_ref.shape[1]
    first = head_ref[0] == 0
    total = sum(t[...].astype(jnp.float32) for t in terms).astype(jnp.bfloat16)
    left, right = total[:, :half], total[:, half:]
    keep_ref[...] = jnp.where(first, left, right)
    send_ref[...] = jnp.where(first, right, left)


def collect(head, mark, terms):
    part, width = terms[0].shape
    return pl.pallas_call(
        functools.partial(collect_kernel, len(terms)),
        out_shape=[jax.ShapeDtypeStruct((part, width // 2), jnp.bfloat16)] * 2,
        in_specs=[pl.BlockSpec(memory_space=pltpu.SMEM), pl.BlockSpec(memory_space=pl.ANY)]
        + [in_vmem()] * len(terms),
        out_specs=[in_vmem()] * 2,
        compiler_params=pltpu.CompilerParams(vmem_limit_bytes=SMALL_LIMIT),
        cost_estimate=NO_COST,
    )(head, mark, *terms)


def place_kernel(head_ref, keep_ref, rest_ref, out_ref):
    part = keep_ref.shape[0]
    first = head_ref[0] == 0
    keep, rest = keep_ref[...], rest_ref[...]
    out_ref[:part] = jnp.where(first, keep, rest)
    out_ref[part:] = jnp.where(first, rest, keep)


def place(head, keep, rest):
    part, half_width = keep.shape
    return pl.pallas_call(
        place_kernel,
        out_shape=jax.ShapeDtypeStruct((2 * part, half_width), jnp.bfloat16),
        in_specs=[pl.BlockSpec(memory_space=pltpu.SMEM)] + [in_vmem()] * 2,
        out_specs=in_vmem(),
        compiler_params=pltpu.CompilerParams(vmem_limit_bytes=SMALL_LIMIT),
        cost_estimate=NO_COST,
    )(head, keep, rest)


def after(mark, *values):
    return lax.optimization_barrier((mark, *values))


def dense_local(tokens, expert_ids, gate_scores, gate_proj, up_proj, down_proj):
    n = lax.axis_size("wide")
    head = lax.axis_index("head").reshape(1)
    expert = lax.axis_index("wide").reshape(1)
    tok_rows, half_width = tokens.shape
    part = tok_rows // 2
    swap = ((0, 1), (1, 0))

    def pair(v):
        return lax.ppermute(v, "wide", [(w, w ^ 1) for w in range(n)])

    def column(v, k):
        return lax.ppermute(v, "wide", [(w, w ^ (2 * k)) for w in range(n)])

    def add(*terms):
        return sum(t.astype(jnp.float32) for t in terms).astype(jnp.bfloat16)

    got = lax.ppermute(tokens, "head", swap)
    mine, lanes, select = spread(head, expert, tokens, expert_ids, gate_scores)
    kept = (gate_proj[0], up_proj[0], down_proj[0])
    lanes, got = after(lanes, got)
    own = join(head, mine, got, lanes)

    last = 2
    mid = list(range(3, n // 2))
    got, *held = after(got, *kept)
    came = [lax.ppermute(w, "head", swap) for w in held]
    block = {0: own}
    block.update({k: column(own, k) for k in mid + [1]})
    over = {}
    over[1] = pair(block[1])
    block[1], own_again = after(block[1], own)
    block[last] = column(own_again, last)
    mark = touch(block[1], *came[:2])
    over[0] = pair(own)
    for k in mid:
        mark, block[k] = after(mark, block[k])
        over[k] = pair(block[k])
    weights, mark = gather_weights(mark, kept, came)
    mark, block[last] = after(mark, block[last])
    over[last] = pair(block[last])

    here, there = {}, {}
    keys = [0] + mid
    groups = [[v[k]] for v in (block, over) for k in keys]
    done, mark = run_expert(mark, groups, select, weights)
    here.update(zip(keys, done))
    for j, k in enumerate(keys):
        there[k] = done[len(keys) + j]
        if k >= 2:
            there[k] = pair(there[k])
    keys = [last] + [1]
    groups = [[v[k]] for v in (block, over) for k in keys]
    done, mark = run_expert(mark, groups, select, weights)
    here.update(zip(keys, done))
    for j, k in enumerate(keys):
        there[k] = done[len(keys) + j]
        if k >= 2:
            there[k] = pair(there[k])
    returned = {}
    for k in mid:
        returned[k] = column(add(here[k], there[k]), k)
        mark = touch(mark, there[k])
    for k in (1, 0):
        mark, there[k] = after(mark, there[k])
        there[k] = pair(there[k])
    returned[last] = column(add(here[last], there[last]), last)
    mark = touch(mark, *[returned[k] for k in mid])
    mark, there[1] = after(mark, there[1])
    returned[1] = column(add(here[1], there[1]), 1)
    terms = [here[0], there[0], *returned.values()]
    keep, send = collect(head, mark, terms)
    rest = lax.ppermute(send, "head", swap)
    return place(head, keep, rest)


def local(tokens, expert_ids, gate_scores, gate_proj, up_proj, down_proj):
    n = lax.axis_size("wide")
    named = expert_ids.shape[1]
    dense = named == n and n >= 8 and n & (n - 1) == 0 and PIECES * n <= LANES
    if dense and lax.axis_size("head") == 2 and tokens.shape[0] % 32 == 0:
        return dense_local(tokens, expert_ids, gate_scores, gate_proj, up_proj, down_proj)
    return sparse_local(tokens, expert_ids, gate_scores, gate_proj, up_proj, down_proj)


def solution(mesh):
    return jax.shard_map(
        local,
        mesh=mesh,
        in_specs=(
            P(("groups", "wide"), "head"),
            P(("groups", "wide"), None),
            P(("groups", "wide"), None),
            P("wide", "head", None),
            P("wide", "head", None),
            P("wide", "head", None),
        ),
        out_specs=P(("groups", "wide"), "head"),
        check_vma=False,
    )
```
